256 devices in a mesh: tile: 32 (over z, y), depth: 8 (over x, core).
Axes of the slice: x: 4, y: 4, z: 8, core: 2. Of those that a mesh axis runs over, the one named last changes fastest.
Arguments:
- phase: float32 [8, 32, 384, 384], P('depth', 'tile'), may hold values from -3.140625 to 3.140625
- absorb: float32 [8, 32, 384, 384], P('depth', 'tile'), may hold values from 0 to 0.3
- probe: float32 [2, 4, 128, 128], replicated, may hold values from -6 to 6
- row_offsets: int32 [32], replicated, may hold values from 0 to 2944
- col_offsets: int32 [32], replicated, may hold values from 0 to 1408
- tile_slot: int32 [32], replicated, may hold values from 0 to 31, each once
- counts: int32 [32, 128, 128], P('tile'), may hold values from 0 to 128
Outputs:
- phase_grad: float32 [8, 32, 384, 384], P('depth', 'tile')
- absorb_grad: float32 [8, 32, 384, 384], P('depth', 'tile')
The draws below stay inside these ranges and needn't reach their ends.
Inputs may be any that keep to these rules, and one draw needn't show every extreme that they name: tile_slot names every storage index once.
All inputs are finite; a program needn't handle non-finite values.
Results may differ from the reference program's by a relative error of at most 0.0003.
Values sent between devices are 32-bit elements; how exact they have to be, the bound alone decides.
A program may use at most 128 MiB of HBM per device.

```python
import math
import jax
import jax.numpy as jnp
from jax import lax

W = 128
MODES = 4
TS = 384
GY = 4
TILES = 32
GX = 8
NROW = 3072
NCOL = 1536
SLICES = 8
POS = 32


def set_ends(result, key, smallest, largest):
    place = [jax.random.randint(jax.random.fold_in(key, axis), (), 0, length) for axis, length in enumerate(result.shape)]
    widest = result.shape.index(max(result.shape))
    neighbour = place[:widest] + [(place[widest] + 1) % result.shape[widest]] + place[widest + 1:]
    return result.at[tuple(place)].set(smallest).at[tuple(neighbour)].set(largest)


def steps_of(own_key, shape, shards, least, top_value):
    loudness = 1.0
    for dim, blocks in shards:
        steps = jax.random.uniform(jax.random.fold_in(jax.random.fold_in(own_key, 6), dim), (blocks,), jnp.float32, least / len(shards), top_value / len(shards))
        loudness = loudness * jnp.repeat(jnp.exp(steps), shape[dim] // blocks).reshape((-1,) + (1,) * (len(shape) - 1 - dim))
    return loudness


def normal_values(stream_key, shape, scale, limit, kind=jnp.bfloat16):
    return jnp.clip(scale * jax.random.normal(stream_key, shape, jnp.float32), -limit, limit).astype(kind)


def setup_inputs(seed: int = 0) -> dict:
    keys = jax.random.split(jax.random.key(seed), 8)
    phase = jnp.clip(jax.random.uniform(keys[0], (SLICES, TILES, TS, TS), jnp.float32, -3.140625, 3.140625), -3.140625, 3.140625)
    absorb = jnp.clip(0.3 * jax.random.uniform(keys[1], (SLICES, TILES, TS, TS), jnp.float32) ** steps_of(keys[1], (SLICES, TILES, TS, TS), ((0, 8), (1, 32)), -0.2, 0.2), 0.0, 0.3)
    probe = normal_values(keys[2], (2, MODES, W, W), 1.0, 6.0, jnp.float32)
    row_offsets = set_ends(jax.random.randint(keys[3], (POS,), 0, NROW - W + 1), jax.random.fold_in(keys[3], 1), 0, NROW - W).astype(jnp.int32)
    col_offsets = set_ends(jax.random.randint(keys[4], (POS,), 0, NCOL - W + 1), jax.random.fold_in(keys[4], 1), 0, NCOL - W).astype(jnp.int32)
    tile_slot = jax.random.permutation(keys[5], TILES).astype(jnp.int32)
    counts = set_ends(jax.random.randint(keys[6], (POS, W, W), 0, 129), jax.random.fold_in(keys[6], 1), 0, 128).astype(jnp.int32)
    return {"phase": phase, "absorb": absorb, "probe": probe, "row_offsets": row_offsets, "col_offsets": col_offsets, "tile_slot": tile_slot, "counts": counts}


count_scale = 0.0078125
loss_scale = 0.03125
fresnel_strength = 40.0

def dft_tables(extent):
    indices = jnp.arange(extent, dtype=jnp.int32)
    phase_steps = indices[:, None] * indices[None, :] % extent
    angles = phase_steps.astype(jnp.float32) * (2.0 * math.pi / extent)
    factor = 1.0 / math.sqrt(extent)
    return (jnp.cos(angles) * factor, -jnp.sin(angles) * factor)

def fresnel(extent):
    indices = jnp.arange(extent, dtype=jnp.int32)
    signed = ((indices + extent // 2) % extent - extent // 2).astype(jnp.float32) / extent
    chirps = fresnel_strength * (signed[:, None] ** 2 + signed[None, :] ** 2)
    return jnp.stack([jnp.cos(chirps), -jnp.sin(chirps)])

def left_times(table, values):
    return jnp.einsum('ij,...jk->...ik', table, values, precision=lax.Precision.HIGHEST)

def right_times(values, table):
    return jnp.einsum('...ij,jk->...ik', values, table, precision=lax.Precision.HIGHEST)

def transform(wave_field, cos_t, sin_t):
    real_in = wave_field[0]
    imag_in = wave_field[1]
    half_real = right_times(real_in, cos_t) - right_times(imag_in, sin_t)
    half_imag = right_times(real_in, sin_t) + right_times(imag_in, cos_t)
    real_out = left_times(cos_t, half_real) - left_times(sin_t, half_imag)
    imag_out = left_times(cos_t, half_imag) + left_times(sin_t, half_real)
    return jnp.stack([real_out, imag_out])

def times_complex(left_op, right_op):
    return jnp.stack([left_op[0] * right_op[0] - left_op[1] * right_op[1], left_op[0] * right_op[1] + left_op[1] * right_op[0]])

def conj_times(left_op, right_op):
    return jnp.stack([left_op[0] * right_op[0] + left_op[1] * right_op[1], left_op[0] * right_op[1] - left_op[1] * right_op[0]])

def propagate(wave_field, tables):
    cos_t, sin_t, kernel = tables
    spectrum = transform(wave_field, cos_t, sin_t)
    return transform(times_complex(kernel, spectrum), cos_t, -sin_t)

def adjoint(wave_field, tables):
    cos_t, sin_t, kernel = tables
    spectrum = transform(wave_field, cos_t, sin_t)
    return transform(conj_times(kernel, spectrum), cos_t, -sin_t)

def reference(phase, absorb, probe, row_offsets, col_offsets, tile_slot, counts):
    cos_t, sin_t = dft_tables(W)
    tables = (cos_t, sin_t, fresnel(W))

    def assemble(layers):
        grid_tiles = jnp.take(layers, tile_slot, axis=1)
        grid_tiles = grid_tiles.reshape(SLICES, GX, GY, TS, TS).transpose(0, 1, 3, 2, 4)
        return grid_tiles.reshape(SLICES, NROW, NCOL)
    regions = jnp.stack([assemble(phase), assemble(absorb)])

    def cut(row_start, col_start):
        zero_idx = jnp.zeros((), jnp.int32)
        return lax.dynamic_slice(regions, (zero_idx, zero_idx, row_start.astype(jnp.int32), col_start.astype(jnp.int32)), (2, SLICES, W, W))
    windows = jax.vmap(cut)(row_offsets, col_offsets)
    damping = jnp.exp(-windows[:, 1])
    trans = jnp.stack([damping * jnp.cos(windows[:, 0]), damping * jnp.sin(windows[:, 0])])
    wave_field = jnp.broadcast_to(probe[:, None], (2, POS, MODES, W, W))
    inputs = []
    for layer_no in range(SLICES):
        inputs.append(wave_field)
        wave_field = propagate(times_complex(trans[:, :, layer_no, None], wave_field), tables)
    far_field = transform(wave_field, cos_t, sin_t)
    intensity = lax.optimization_barrier(jnp.sum(far_field[0] ** 2 + far_field[1] ** 2, axis=1))
    residual = intensity - count_scale * counts.astype(jnp.float32)
    back_field = 4.0 * loss_scale * residual[None, :, None] * far_field
    gradient = transform(back_field, cos_t, -sin_t)
    pieces = [None] * SLICES
    for layer_no in reversed(range(SLICES)):
        arriving = adjoint(gradient, tables)
        pieces[layer_no] = lax.optimization_barrier(jnp.sum(conj_times(inputs[layer_no], arriving), axis=2))
        gradient = conj_times(trans[:, :, layer_no, None], arriving)
    object_grad = jnp.stack(pieces, 2)
    phase_part = trans[0] * object_grad[1] - trans[1] * object_grad[0]
    absorb_part = -(trans[0] * object_grad[0] + trans[1] * object_grad[1])
    window_grads = jnp.stack([phase_part, absorb_part], 1)

    def deposit(position, total):
        zero_idx = jnp.zeros((), jnp.int32)
        row_start = row_offsets[position].astype(jnp.int32)
        col_start = col_offsets[position].astype(jnp.int32)
        where_at = (zero_idx, zero_idx, row_start, col_start)
        current = lax.dynamic_slice(total, where_at, (2, SLICES, W, W))
        return lax.dynamic_update_slice(total, current + window_grads[position], where_at)
    total = lax.fori_loop(0, POS, deposit, jnp.zeros((2, SLICES, NROW, NCOL), jnp.float32))
    grid_tiles = total.reshape(2, SLICES, GX, TS, GY, TS).transpose(0, 1, 2, 4, 3, 5).reshape(2, SLICES, TILES, TS, TS)
    stored_tiles = jnp.zeros_like(grid_tiles).at[:, :, tile_slot].set(grid_tiles)
    return (stored_tiles[0], stored_tiles[1])
```

```python
import functools
import math

import numpy as np
import jax
import jax.numpy as jnp
from jax import lax
from jax.experimental import pallas as pl
from jax.experimental.pallas import tpu as pltpu
from jax.sharding import PartitionSpec as P

W = 128
MODES = 4
TS = 384
GY = 4
POS = 32
NZ = 8
NY = 4
DEPTH = 8
CHUNKS = TS // W + 2
PADDED = TS + 2 * W

count_scale = 0.0078125
loss_scale = 0.03125
fresnel_strength = 40.0

VMEM = pl.BlockSpec(memory_space=pltpu.VMEM)
SMEM = pl.BlockSpec(memory_space=pltpu.SMEM)
ANY = pl.BlockSpec(memory_space=pl.ANY)
MESH = pl.DeviceIdType.MESH


def make_tables():
    index = np.arange(W)
    angle = 2.0 * np.pi * ((index[:, None] * index[None, :]) % W) / W
    dft = np.exp(-1j * angle) / math.sqrt(W)
    signed = ((index + W // 2) % W - W // 2) / W
    chirp = np.exp(-1j * fresnel_strength * signed**2)
    step = np.conj(dft) @ (chirp[:, None] * dft)
    tables = []
    for g in (step, dft):
        right = np.block([[g.real, g.imag], [-g.imag, g.real]])
        for table in (right, right.T):
            table = table.astype(np.float32)
            high = table.astype(jnp.bfloat16)
            low = (table - high.astype(np.float32)).astype(jnp.bfloat16)
            tables.append(np.stack([high, low]))
    return np.stack(tables)


def tile_corner(slots, me):
    def look(i, place):
        return jnp.where(slots[i] == me, i, place)

    place = lax.fori_loop(0, POS, look, jnp.int32(0))
    row = place // GY
    return row * TS, (place - row * GY) * TS


def overlap(rows, cols, p, top, left):
    dr = rows[p] - top
    dc = cols[p] - left
    return dr, dc, (dr > -W) & (dr < TS) & (dc > -W) & (dc < TS)


def extract_kernel(rows, cols, slots, phase, absorb, out, padded):
    me = lax.axis_index("tile")
    top, left = tile_corner(slots, me)
    padded[...] = jnp.zeros_like(padded)
    for m, source in enumerate((phase, absorb)):
        for c in range(CHUNKS - 2):
            padded[m, c + 1, W : W + TS, :] = source[0, 0, :, c * W : (c + 1) * W]
    lane = lax.broadcasted_iota(jnp.int32, (W, W), 1)

    def one(p, carry):
        dr, dc, touches = overlap(rows, cols, p, top, left)

        @pl.when(touches)
        def _():
            start = dr + W
            chunk = (dc + W) // W
            shift = dc + W - chunk * W
            turn = jnp.where(shift == 0, 0, W - shift)
            for m in range(2):
                first = padded[m, chunk, pl.ds(start, W), :]
                second = padded[m, chunk + 1, pl.ds(start, W), :]
                out[p, m] = jnp.where(
                    lane < W - shift, pltpu.roll(first, turn, 1), pltpu.roll(second, turn, 1)
                )

        @pl.when(jnp.logical_not(touches))
        def _():
            out[p] = jnp.zeros((2, W, W), jnp.float32)

        return carry

    lax.fori_loop(0, POS, one, 0)


def deposit_kernel(rows, cols, slots, grads, phase_out, absorb_out, acc, held, sems):
    me = lax.axis_index("tile")
    top, left = tile_corner(slots, me)

    def fetch(p):
        return pltpu.make_async_copy(grads.at[p], held.at[p], sems.at[p])

    def begin(p, carry):
        dr, dc, touches = overlap(rows, cols, p, top, left)

        @pl.when(touches)
        def _():
            fetch(p).start()

        return carry

    lax.fori_loop(0, POS, begin, 0)
    acc[...] = jnp.zeros_like(acc)
    lane = lax.broadcasted_iota(jnp.int32, (W, W), 1)

    def one(p, carry):
        dr, dc, touches = overlap(rows, cols, p, top, left)

        @pl.when(touches)
        def _():
            fetch(p).wait()
            start = dr + W
            chunk = (dc + W) // W
            shift = dc + W - chunk * W
            for m in range(2):
                turned = pltpu.roll(held[p, m], shift, 1)
                acc[m, chunk, pl.ds(start, W), :] += jnp.where(lane >= shift, turned, 0.0)
                acc[m, chunk + 1, pl.ds(start, W), :] += jnp.where(lane < shift, turned, 0.0)

        return carry

    lax.fori_loop(0, POS, one, 0)
    for m, target in enumerate((phase_out, absorb_out)):
        for c in range(CHUNKS - 2):
            target[0, 0, :, c * W : (c + 1) * W] = acc[m, c + 1, W : W + TS, :]


def tile_place():
    me = lax.axis_index("tile")
    z = me // NY
    return z, me - z * NY


def turned(value, step, count):
    return lax.rem(value + step + count, count)


def greet(partners):
    barrier = pltpu.get_barrier_semaphore()
    for partner in partners:
        pl.semaphore_signal(barrier, inc=1, device_id=partner, device_id_type=MESH)
    pl.semaphore_wait(barrier, len(partners))


def tile_partners(z, y):
    return [
        {"tile": turned(z, 1, NZ) * NY + y},
        {"tile": turned(z, -1, NZ) * NY + y},
        {"tile": z * NY + turned(y, 1, NY)},
        {"tile": z * NY + turned(y, -1, NY)},
        {"tile": z * NY + turned(y, 2, NY)},
    ]


class Sender:
    def __init__(self, send_sems, recv_sems):
        self.send_sems, self.recv_sems = send_sems, recv_sems
        self.used = 0
        self.started = []

    def copy(self, source, target, device):
        n = self.used
        self.used += 1
        copy = pltpu.make_async_remote_copy(
            src_ref=source,
            dst_ref=target,
            send_sem=self.send_sems.at[n],
            recv_sem=self.recv_sems.at[n],
            device_id=device,
            device_id_type=MESH,
        )
        copy.start()
        self.started.append(copy)
        return copy

    def finish(self):
        for copy in self.started:
            copy.wait_send()


def ring_streams(count, streams):
    plan = []
    for stream in range(streams):
        first = stream < streams // 2
        plan.append((stream, 1, count // 2 if first else count // 2 - 1))
        plan.append((stream, -1, count // 2 - 1 if first else count // 2))
    return plan


SCATTER_COPIES = 28 + 3 + 24 + 14
HALF = W // 2


def scatter_kernel(ext, out, a_recv, a_side, b_recv, b_recv2, send_sems, recv_sems):
    z, y = tile_place()
    greet(tile_partners(z, y))
    send = Sender(send_sems, recv_sems)

    def z_device(way):
        return {"tile": turned(z, way, NZ) * NY + y}

    def y_device(step):
        return {"tile": z * NY + turned(y, step, NY)}

    a_last = {}
    a_slot = [0]

    def a_step(s):
        for stream, way, length in ring_streams(NZ, NY):
            if s >= length:
                continue
            dest = turned(z, way * (length - s), NZ) * NY + stream
            if s > 0:
                copy, slot = a_last[stream, way]
                copy.wait_recv()
                a_recv[slot] += ext[dest, 0]
                source = a_recv.at[slot]
            else:
                source = ext.at[dest, 0]
            slot = a_slot[0]
            a_slot[0] += 1
            copy = send.copy(source, a_recv.at[slot], z_device(way))
            a_last[stream, way] = (copy, slot)

    b_last = {}
    b_slot = [0]

    def b_step(s):
        for stream in range(NZ):
            for way in (1, -1):
                length = 2 if (stream % 2 == 0) == (way == 1) else 1
                if s >= length:
                    continue
                dest = stream * NY + turned(y, way * (length - s), NY)
                if s > 0:
                    copy, slot = b_last[stream, way]
                    copy.wait_recv()
                    b_recv[slot] += ext[dest, 1]
                    source = b_recv.at[slot]
                else:
                    source = ext.at[dest, 1]
                slot = b_slot[0]
                b_slot[0] += 1
                copy = send.copy(source, b_recv.at[slot], y_device(way))
                b_last[stream, way] = (copy, slot)

    a_step(0)
    b_step(0)
    a_step(1)
    b_step(1)
    a_step(2)
    for stream in range(NZ):
        mine = stream * NY + y
        total = ext[mine, 1]
        for way in (1, -1):
            copy, slot = b_last[stream, way]
            copy.wait_recv()
            total = total + b_recv[slot]
        b_recv2[stream] = total
    c_last = {}
    c_slot = [0]

    def c_step(s):
        for stream, way, length in ring_streams(NZ, 2):
            if s >= length:
                continue
            dest = turned(z, way * (length - s), NZ)
            part = pl.ds(stream * HALF, HALF)
            if s > 0:
                copy, slot = c_last[stream, way]
                copy.wait_recv()
                b_recv2[NZ + slot, :HALF] += b_recv2[dest, part]
                source = b_recv2.at[NZ + slot, pl.ds(0, HALF)]
            else:
                source = b_recv2.at[dest, part]
            slot = c_slot[0]
            c_slot[0] += 1
            copy = send.copy(source, b_recv2.at[NZ + slot, pl.ds(0, HALF)], z_device(way))
            c_last[stream, way] = (copy, slot)

    c_step(0)
    a_step(3)
    c_step(1)
    a_copies = []
    for stream in range(NY):
        mine = z * NY + stream
        total = ext[mine, 0]
        for way in (1, -1):
            copy, slot = a_last[stream, way]
            copy.wait_recv()
            total = total + a_recv[slot]
        a_side[stream] = total
    for step in (1, 2, 3):
        a_copies.append(
            send.copy(a_side.at[turned(y, step, NY)], a_side.at[NY + step], y_device(step))
        )
    c_step(2)
    c_step(3)
    total = a_side[y]
    for step, copy in zip((1, 2, 3), a_copies):
        copy.wait_recv()
        total = total + a_side[NY + step]
    out[0] = total
    for stream in range(2):
        part = pl.ds(stream * HALF, HALF)
        total = b_recv2[z, part]
        for way in (1, -1):
            copy, slot = c_last[stream, way]
            copy.wait_recv()
            total = total + b_recv2[NZ + slot, :HALF]
        out[1, part] = total
    send.finish()


GATHER_COPIES = 14 + 24 + 3 + 28


def gather_kernel(own, out, send_sems, recv_sems):
    z, y = tile_place()
    greet(tile_partners(z, y))
    send = Sender(send_sems, recv_sems)
    me = z * NY + y

    def z_device(way):
        return {"tile": turned(z, way, NZ) * NY + y}

    def y_device(step):
        return {"tile": z * NY + turned(y, step, NY)}

    out[me] = own[...]

    b_copies = {0: None}
    for step in (1, 3, 2):
        b_copies[step] = send.copy(out.at[me, 1], out.at[me, 1], y_device(step))

    c_last = {}

    def c_step(s):
        for stream, way, length in ring_streams(NZ, 2):
            chunk = turned(z, -way * s, NZ) * NY + y
            part = pl.ds(stream * HALF, HALF)
            if s > 0:
                c_last[stream, way].wait_recv()
            if s >= length:
                continue
            c_last[stream, way] = send.copy(
                out.at[chunk, 0, part], out.at[chunk, 0, part], z_device(way)
            )

    a_last = {}

    def a_step(s):
        for stream, way, length in ring_streams(NZ, NY):
            if s >= length:
                continue
            column = turned(y, -stream, NY)
            chunk = turned(z, -way * s, NZ) * NY + column
            if s > 0:
                a_last[stream, way].wait_recv()
            elif way == 1 and b_copies[stream] is not None:
                b_copies[stream].wait_recv()
            a_last[stream, way] = send.copy(out.at[chunk, 1], out.at[chunk, 1], z_device(way))

    b_last = {}

    def b_first(offset):
        for way in (1, -1):
            chunk = turned(z, offset, NZ) * NY + y
            b_last[offset % NZ, way] = send.copy(out.at[chunk, 0], out.at[chunk, 0], y_device(way))

    def b_second(offset):
        offset = offset % NZ
        way = 1 if offset % 2 == 0 else -1
        b_last[offset, way].wait_recv()
        chunk = turned(z, offset, NZ) * NY + turned(y, -way, NY)
        b_last[offset, 2] = send.copy(out.at[chunk, 0], out.at[chunk, 0], y_device(way))

    c_step(0)
    b_first(0)
    a_step(0)
    for s in range(1, NZ // 2):
        c_step(s)
        b_first(-s)
        b_first(s)
        a_step(s)
        b_second(s - 1)
        if s > 1:
            b_second(1 - s)
    c_last[0, 1].wait_recv()
    c_last[1, -1].wait_recv()
    b_first(NZ // 2)
    b_second(NZ // 2 - 1)
    b_second(1 - NZ // 2)
    b_second(NZ // 2)
    for offset in range(NZ):
        forwarded = 1 if offset % 2 == 0 else -1
        b_last[offset, -forwarded].wait_recv()
        b_last[offset, 2].wait_recv()
    for stream, way, length in ring_streams(NZ, NY):
        a_last[stream, way].wait_recv()
    send.finish()


def split(value):
    high = value.astype(jnp.bfloat16)
    low = (value - high.astype(jnp.float32)).astype(jnp.bfloat16)
    return high, low


def mxu(a, b):
    return jnp.dot(a, b, preferred_element_type=jnp.float32)


def transform(real, imag, tables, right, left):
    high, low = split(jnp.concatenate([real, imag], 1))
    half = mxu(high, tables[right, 0]) + (mxu(low, tables[right, 0]) + mxu(high, tables[right, 1]))
    high, low = split(jnp.concatenate([half[:, :W], half[:, W:]], 0))
    done = mxu(tables[left, 0], jnp.concatenate([high, low], 1))
    done = done[:, :W] + (done[:, W:] + mxu(tables[left, 1], high))
    return done[:W], done[W:]


STEP, STEP_BACK, DFT, DFT_BACK = (0, 1), (1, 0), (2, 3), (3, 2)


def chain_kernel(
    windows, probe, counts, tables, out,
    trans, waves, shares, grads, got,
    t_send, t_recv, i_send, i_recv, g_send, g_recv,
):
    d = lax.axis_index("depth")
    x = d // 2
    core = d - x * 2
    greet([{"depth": turned(d, k, DEPTH)} for k in range(1, DEPTH)])

    damping = jnp.exp(-windows[1])
    trans[d, 0] = damping * jnp.cos(windows[0])
    trans[d, 1] = damping * jnp.sin(windows[0])

    def trans_copy(k):
        return pltpu.make_async_remote_copy(
            src_ref=trans.at[d],
            dst_ref=trans.at[d],
            send_sem=t_send.at[k],
            recv_sem=t_recv.at[d],
            device_id={"depth": turned(x, k, MODES) * 2},
            device_id_type=MESH,
        )

    for k in (1, 3, 2):
        trans_copy(k).start()

    @pl.when(core == 1)
    def _():
        trans_copy(0).start()

    def share_copy(k):
        return pltpu.make_async_remote_copy(
            src_ref=shares.at[0],
            dst_ref=shares.at[k],
            send_sem=i_send.at[k],
            recv_sem=i_recv.at[k],
            device_id={"depth": turned(x, k, MODES) * 2},
            device_id_type=MESH,
        )

    def grad_copy(j):
        return pltpu.make_async_remote_copy(
            src_ref=grads.at[j],
            dst_ref=got.at[x],
            send_sem=g_send.at[j],
            recv_sem=g_recv.at[x],
            device_id={"depth": j},
            device_id_type=MESH,
        )

    @pl.when(core == 0)
    def _():
        real, imag = probe[0, x], probe[1, x]
        for j in range(DEPTH):
            waves[j, 0] = real
            waves[j, 1] = imag

            @pl.when(d != j)
            def _():
                pltpu.make_async_remote_copy(
                    src_ref=trans.at[j],
                    dst_ref=trans.at[j],
                    send_sem=t_send.at[0],
                    recv_sem=t_recv.at[j],
                    device_id={"depth": turned(d, 1, DEPTH)},
                    device_id_type=MESH,
                ).wait_recv()

            tr, ti = trans[j, 0], trans[j, 1]
            table = STEP if j < DEPTH - 1 else DFT
            real, imag = transform(
                tr * real - ti * imag, tr * imag + ti * real, tables, *table
            )
        shares[0] = real * real + imag * imag
        for k in (1, 3, 2):
            share_copy(k).start()
        residual = shares[0] - count_scale * counts[0].astype(jnp.float32)
        for k in (1, 3, 2):
            share_copy(k).wait_recv()
            residual = residual + shares[k]
        residual = (4.0 * loss_scale) * residual
        real, imag = residual * real, residual * imag
        for j in reversed(range(DEPTH)):
            table = STEP_BACK if j < DEPTH - 1 else DFT_BACK
            real, imag = transform(real, imag, tables, *table)
            tr, ti = trans[j, 0], trans[j, 1]
            real, imag = tr * real + ti * imag, tr * imag - ti * real
            wr, wi = waves[j, 0], waves[j, 1]
            grads[j, 0] = wr * imag - wi * real
            grads[j, 1] = -(wr * real + wi * imag)

            @pl.when(d != j)
            def _():
                grad_copy(j).start()

            @pl.when(d == j)
            def _():
                got[x] = grads[j]

        for k in (1, 3, 2):
            share_copy(k).wait_send()
        for j in range(DEPTH):

            @pl.when(d != j)
            def _():
                grad_copy(j).wait_send()

    for k in (1, 3, 2):
        trans_copy(k).wait_send()

    @pl.when(core == 1)
    def _():
        trans_copy(0).wait_send()

    for k in range(MODES):

        @pl.when(d != 2 * k)
        def _():
            pltpu.make_async_remote_copy(
                src_ref=got.at[k],
                dst_ref=got.at[k],
                send_sem=g_send.at[0],
                recv_sem=g_recv.at[k],
                device_id={"depth": turned(d, 1, DEPTH)},
                device_id_type=MESH,
            ).wait_recv()

    out[...] = (got[0] + got[1]) + (got[2] + got[3])


def local(phase, absorb, probe, row_offsets, col_offsets, tile_slot, counts):
    f32 = jnp.float32
    mib = 1 << 20
    dma = pltpu.SemaphoreType.DMA
    parts = pl.pallas_call(
        extract_kernel,
        out_shape=jax.ShapeDtypeStruct((POS, 2, W, W), f32),
        in_specs=[SMEM, SMEM, SMEM, VMEM, VMEM],
        out_specs=VMEM,
        scratch_shapes=[pltpu.VMEM((2, CHUNKS, PADDED, W), f32)],
        compiler_params=pltpu.CompilerParams(vmem_limit_bytes=24 * mib),
        name="extract",
    )(row_offsets, col_offsets, tile_slot, phase, absorb)
    windows = pl.pallas_call(
        scatter_kernel,
        out_shape=jax.ShapeDtypeStruct((2, W, W), f32),
        in_specs=[VMEM],
        out_specs=VMEM,
        scratch_shapes=[
            pltpu.VMEM((28, W, W), f32),
            pltpu.VMEM((2 * NY, W, W), f32),
            pltpu.VMEM((24, W, W), f32),
            pltpu.VMEM((NZ + 14, W, W), f32),
            dma((SCATTER_COPIES,)),
            dma((SCATTER_COPIES,)),
        ],
        compiler_params=pltpu.CompilerParams(
            collective_id=0, has_side_effects=True, vmem_limit_bytes=24 * mib
        ),
        name="scatter",
    )(parts)
    grads = pl.pallas_call(
        chain_kernel,
        out_shape=jax.ShapeDtypeStruct((2, W, W), f32),
        in_specs=[VMEM] * 4,
        out_specs=VMEM,
        scratch_shapes=[
            pltpu.VMEM((DEPTH, 2, W, W), f32),
            pltpu.VMEM((DEPTH, 2, W, W), f32),
            pltpu.VMEM((MODES, W, W), f32),
            pltpu.VMEM((DEPTH, 2, W, W), f32),
            pltpu.VMEM((MODES, 2, W, W), f32),
            dma((MODES,)),
            dma((DEPTH,)),
            dma((MODES,)),
            dma((MODES,)),
            dma((DEPTH,)),
            dma((MODES,)),
        ],
        compiler_params=pltpu.CompilerParams(
            collective_id=1, has_side_effects=True, vmem_limit_bytes=24 * mib
        ),
        name="chain",
    )(windows, probe, counts, jnp.asarray(make_tables()))
    gathered = pl.pallas_call(
        gather_kernel,
        out_shape=jax.ShapeDtypeStruct((POS, 2, W, W), f32),
        in_specs=[VMEM],
        out_specs=VMEM,
        scratch_shapes=[dma((GATHER_COPIES,)), dma((GATHER_COPIES,))],
        compiler_params=pltpu.CompilerParams(
            collective_id=2, has_side_effects=True, vmem_limit_bytes=24 * mib
        ),
        name="gather",
    )(grads)
    return pl.pallas_call(
        deposit_kernel,
        out_shape=(jax.ShapeDtypeStruct((1, 1, TS, TS), f32),) * 2,
        in_specs=[SMEM, SMEM, SMEM, ANY],
        out_specs=(VMEM, VMEM),
        scratch_shapes=[
            pltpu.VMEM((2, CHUNKS, PADDED, W), f32),
            pltpu.VMEM((POS, 2, W, W), f32),
            dma((POS,)),
        ],
        compiler_params=pltpu.CompilerParams(vmem_limit_bytes=24 * mib),
        name="deposit",
    )(row_offsets, col_offsets, tile_slot, gathered)


def solution(mesh):
    in_specs = (
        P("depth", "tile", None, None),
        P("depth", "tile", None, None),
        P(),
        P(),
        P(),
        P(),
        P("tile", None, None),
    )
    out_specs = (P("depth", "tile", None, None), P("depth", "tile", None, None))
    return jax.shard_map(local, mesh=mesh, in_specs=in_specs, out_specs=out_specs, check_vma=False)
```

```python
import functools
import math

import numpy as np
import jax
import jax.numpy as jnp
from jax import lax
from jax.experimental import pallas as pl
from jax.experimental.pallas import tpu as pltpu
from jax.sharding import PartitionSpec as P

W = 128
MODES = 4
TS = 384
GY = 4
POS = 32
NZ = 8
NY = 4
DEPTH = 8
BOTH = 2 * W
ROWS_A = 96
ROWS_B = BOTH - ROWS_A
HALF_B = ROWS_B // 2
CHUNKS = TS // W + 2
PADDED = TS + 2 * W

count_scale = 0.0078125
loss_scale = 0.03125
fresnel_strength = 40.0

VMEM = pl.BlockSpec(memory_space=pltpu.VMEM)
SMEM = pl.BlockSpec(memory_space=pltpu.SMEM)
HBM = pl.BlockSpec(memory_space=pltpu.HBM)
ANY = pl.BlockSpec(memory_space=pl.ANY)
MESH = pl.DeviceIdType.MESH


def make_tables():
    index = np.arange(W)
    angle = 2.0 * np.pi * ((index[:, None] * index[None, :]) % W) / W
    dft = np.exp(-1j * angle) / math.sqrt(W)
    signed = ((index + W // 2) % W - W // 2) / W
    chirp = np.exp(-1j * fresnel_strength * signed**2)
    step = np.conj(dft) @ (chirp[:, None] * dft)
    tables = []
    for g in (step, dft):
        right = np.block([[g.real, g.imag], [-g.imag, g.real]])
        for table in (right, right.T):
            table = table.astype(np.float32)
            high = table.astype(jnp.bfloat16)
            low = (table - high.astype(np.float32)).astype(jnp.bfloat16)
            tables.append(np.stack([high, low]))
    return np.stack(tables)


def tile_corner(slots, me):
    def look(i, place):
        return jnp.where(slots[i] == me, i, place)

    place = lax.fori_loop(0, POS, look, jnp.int32(0))
    row = lax.shift_right_logical(place, 2)
    return row * TS, (place - row * GY) * TS


def overlap(rows, cols, p, top, left):
    dr = rows[p] - top
    dc = cols[p] - left
    return dr, dc, (dr > -W) & (dr < TS) & (dc > -W) & (dc < TS)


def deposit_kernel(rows, cols, slots, grads, phase_out, absorb_out, acc, held, sems):
    me = lax.axis_index("tile")
    top, left = tile_corner(slots, me)

    z, y = tile_place()

    def fetch(p):
        row = lax.shift_right_logical(p, 2)
        place = turned(row, -z, NZ) * NY + turned(p - row * NY, -y, NY)
        return pltpu.make_async_copy(grads.at[place], held.at[p], sems.at[p])

    def begin(p, carry):
        dr, dc, touches = overlap(rows, cols, p, top, left)

        @pl.when(touches)
        def _():
            fetch(p).start()

        return carry

    lax.fori_loop(0, POS, begin, 0)
    acc[...] = jnp.zeros_like(acc)
    lane = lax.broadcasted_iota(jnp.int32, (W, W), 1)

    def one(p, carry):
        dr, dc, touches = overlap(rows, cols, p, top, left)

        @pl.when(touches)
        def _():
            fetch(p).wait()
            start = dr + W
            chunk = lax.shift_right_logical(dc + W, 7)
            shift = dc + W - chunk * W
            for m in range(2):
                moved = pltpu.roll(held[p, m * W : (m + 1) * W], shift, 1)
                acc[m, chunk, pl.ds(start, W), :] += jnp.where(lane >= shift, moved, 0.0)
                acc[m, chunk + 1, pl.ds(start, W), :] += jnp.where(lane < shift, moved, 0.0)

        return carry

    lax.fori_loop(0, POS, one, 0)
    for m, target in enumerate((phase_out, absorb_out)):
        for c in range(TS // W):
            target[0, 0, :, c * W : (c + 1) * W] = acc[m, c + 1, W : W + TS, :]


def tile_place():
    me = lax.axis_index("tile")
    z = me // NY
    return z, me - z * NY


def turned(value, step, count):
    return lax.rem(value + step + count, count)


def z_device(way):
    z, y = tile_place()
    return {"tile": turned(z, way, NZ) * NY + y}


def y_device(step):
    z, y = tile_place()
    return {"tile": z * NY + turned(y, step, NY)}


def tile_partners():
    return [z_device(k) for k in (1, -1, 2, -2)] + [y_device(k) for k in range(1, NY)]


class Sender:
    def __init__(self, send_sems, recv_sems):
        self.send_sems, self.recv_sems = send_sems, recv_sems
        self.started = []

    def copy(self, source, target, device):
        n = len(self.started)
        copy = pltpu.make_async_remote_copy(
            src_ref=source,
            dst_ref=target,
            send_sem=self.send_sems.at[n],
            recv_sem=self.recv_sems.at[n],
            device_id=device,
            device_id_type=MESH,
        )
        copy.start()
        self.started.append(copy)
        return copy

    def finish(self):
        for copy in self.started:
            copy.wait_send()


HOPS4 = ((0, 1), (1, 1), (2, -1), (3, -1))
HOPS3 = ((2, 1), (3, 1), (0, -1), (1, -1))
SCATTER_COPIES = 28 + 3 + 24 + 8
GATHER_COPIES = 28 + 3 + 24 + 8
FAR_FIRST = (4, 3, -3, 2, -2, 1, -1, 0)
PART_A = pl.ds(0, ROWS_A)
PART_B = pl.ds(ROWS_A, ROWS_B)
ALL_B = pl.ds(0, ROWS_B)


def half_of(way):
    return 0 if way == 1 else HALF_B


def spot(dz, dy):
    return (dz % NZ) * NY + dy % NY


def scatter(extract, ready, ext, out, a_recv, a_side, b_recv, b_sum, c_recv, send):
    a_last, b_last, c_last = {}, {}, {}
    a_slots, b_slots = iter(range(28)), iter(range(24))

    def a_step(streams, length, s):
        for stream, way in streams:
            dest = spot(way * (length - s), stream)
            if s > 0:
                copy, slot = a_last[stream, way]
                copy.wait_recv()
                a_recv[slot] += ext[dest, PART_A]
                source = a_recv.at[slot]
            else:
                source = ext.at[dest, PART_A]
            slot = next(a_slots)
            a_last[stream, way] = (send.copy(source, a_recv.at[slot], z_device(way)), slot)

    def b_send(offset, way, source):
        slot = next(b_slots)
        b_last[offset, way] = (send.copy(source, b_recv.at[slot], y_device(way)), slot)

    def b_far(offset):
        way = 1 if offset % 2 == 0 else -1
        b_send(offset, way, ext.at[spot(offset, 2), PART_B])
        b_send(offset, -way, ext.at[spot(offset, -way), PART_B])

    def b_near(offset):
        way = 1 if offset % 2 == 0 else -1
        copy, slot = b_last[offset, way]
        copy.wait_recv()
        b_recv[slot] += ext[spot(offset, way), PART_B]
        b_send(offset, way, b_recv.at[slot])

    def b_total(offset):
        total = ext[spot(offset, 0), PART_B]
        for way in (1, -1):
            copy, slot = b_last[offset, way]
            copy.wait_recv()
            total = total + b_recv[slot]
        b_sum[offset % NZ] = total

    def c_slot(away, way):
        return 2 * (away - 1) + (way < 0)

    def c_send(away, way, source, part, hops):
        target = c_recv.at[c_slot(away, way), part]
        c_last[away, way] = send.copy(source, target, z_device(way * hops))

    def c_far():
        for way in (1, -1):
            part = pl.ds(half_of(way), HALF_B)
            c_send(4, way, b_sum.at[4, part], part, 2)
        for way in (1, -1):
            c_send(3, way, b_sum.at[3 * way % NZ], ALL_B, 1)

    def c_two(way):
        c_last[3, way].wait_recv()
        c_last[4, way].wait_recv()
        slot = c_slot(3, way)
        part = pl.ds(half_of(way), HALF_B)
        c_recv[slot] += b_sum[2 * way % NZ]
        c_recv[slot, part] += c_recv[c_slot(4, way), part]
        c_send(2, way, c_recv.at[slot], ALL_B, 2)

    def c_one(way):
        c_send(1, way, b_sum.at[way % NZ], ALL_B, 1)

    extract(4)
    ready()
    a_step(HOPS4, 4, 0)
    b_far(4)
    extract(3)
    a_step(HOPS3[:2], 3, 0)
    extract(-3)
    a_step(HOPS3[2:], 3, 0)
    b_far(3)
    extract(2)
    extract(-2)
    b_far(-3)
    a_step(HOPS4, 4, 1)
    b_near(4)
    b_far(2)
    extract(1)
    extract(-1)
    a_step(HOPS3, 3, 1)
    b_near(3)
    b_far(-2)
    extract(0)
    a_step(HOPS4, 4, 2)
    b_near(-3)
    b_far(1)
    b_total(4)
    a_step(HOPS3, 3, 2)
    b_near(2)
    b_far(-1)
    b_total(3)
    b_total(-3)
    c_far()
    a_step(HOPS4, 4, 3)
    b_near(-2)
    b_far(0)
    b_total(2)
    b_near(1)
    b_total(-2)
    for stream in range(NY):
        total = ext[spot(0, stream), PART_A]
        for way in (1, -1):
            copy, slot = a_last[stream, way]
            copy.wait_recv()
            total = total + a_recv[slot]
        a_side[stream] = total
    a_copies = [
        send.copy(a_side.at[step], a_side.at[NY + step], y_device(step)) for step in (1, 3, 2)
    ]
    c_two(1)
    c_two(-1)
    b_near(-1)
    b_total(1)
    c_one(1)
    b_near(0)
    b_total(-1)
    c_one(-1)
    b_total(0)
    total = a_side[0]
    for step, copy in zip((1, 3, 2), a_copies):
        copy.wait_recv()
        total = total + a_side[NY + step]
    out[PART_A] = total
    total = b_sum[0]
    for away in (2, 1):
        for way in (1, -1):
            c_last[away, way].wait_recv()
            total = total + c_recv[c_slot(away, way)]
    out[PART_B] = total


def gather(out, send):
    a_last, b_last, c_last = {}, {}, {}

    def z_copy(dz, dy, part, way):
        source, target = out.at[spot(dz, dy), part], out.at[spot(dz - way, dy), part]
        return send.copy(source, target, z_device(way))

    def y_copy(dz, dy, part, way):
        source, target = out.at[spot(dz, dy), part], out.at[spot(dz, dy - way), part]
        return send.copy(source, target, y_device(way))

    def a_first():
        for step in (1, 3, 2):
            a_last[step] = y_copy(0, 0, PART_A, step)

    def a_step(s, streams):
        if s == 0:
            for stream in streams:
                if stream > 0:
                    a_last[stream].wait_recv()
        for found, length in ((HOPS4, 4), (HOPS3, 3)):
            for stream, way in found:
                if s >= length or stream not in streams:
                    continue
                if s > 0:
                    a_last[stream, way].wait_recv()
                a_last[stream, way] = z_copy(-way * s, -stream, PART_A, way)

    def c_near():
        for away in (1, 2):
            for way in (1, -1):
                c_last[away, way] = z_copy(0, 0, PART_B, way * away)

    def c_far(way):
        c_last[2, way].wait_recv()
        c_last[3, way] = z_copy(-2 * way, 0, PART_B, way)
        part = pl.ds(ROWS_A + half_of(way), HALF_B)
        c_last[4, way] = z_copy(-2 * way, 0, part, 2 * way)

    def b_first(offset):
        for way in (1, -1):
            b_last[offset, way] = y_copy(offset, 0, PART_B, way)

    def b_second(offset):
        way = 1 if offset % 2 == 0 else -1
        b_last[offset, way].wait_recv()
        b_last[offset, 2] = y_copy(offset, -way, PART_B, way)

    c_near()
    a_first()
    b_first(0)
    a_step(0, (0,))
    for way in (1, -1):
        c_last[1, way].wait_recv()
        b_first(-way)
    a_step(0, (1,))
    a_step(0, (3,))
    b_second(0)
    c_far(1)
    c_far(-1)
    b_first(-2)
    b_first(2)
    a_step(0, (2,))
    a_step(1, (0,))
    b_second(1)
    b_second(-1)
    a_step(1, (1,))
    a_step(1, (3,))
    for way in (1, -1):
        c_last[3, way].wait_recv()
        b_first(-3 * way)
    a_step(1, (2,))
    b_second(2)
    b_second(-2)
    a_step(2, (0,))
    for way in (1, -1):
        c_last[4, way].wait_recv()
    b_first(4)
    a_step(2, (1,))
    a_step(2, (3,))
    b_second(3)
    b_second(-3)
    a_step(2, (2,))
    a_step(3, (0,))
    b_second(4)
    a_step(3, (1, 3, 2))
    for offset in FAR_FIRST:
        forwarded = 1 if offset % 2 == 0 else -1
        b_last[offset, -forwarded].wait_recv()
        b_last[offset, 2].wait_recv()
    for stream, way in HOPS4 + HOPS3:
        a_last[stream, way].wait_recv()


def split(value):
    high = value.astype(jnp.bfloat16)
    low = (value - high.astype(jnp.float32)).astype(jnp.bfloat16)
    return high, low


def mxu(a, b):
    return jnp.dot(a, b, preferred_element_type=jnp.float32)


def transform(fields, tables, right, left):
    count = len(fields)
    high, low = split(jnp.concatenate([jnp.concatenate(field, 1) for field in fields], 0))
    half = mxu(high, tables[right, 0]) + (mxu(low, tables[right, 0]) + mxu(high, tables[right, 1]))
    blocks = [half[m * W : (m + 1) * W] for m in range(count)]
    half = jnp.concatenate(
        [
            jnp.concatenate([block[:, :W] for block in blocks], 1),
            jnp.concatenate([block[:, W:] for block in blocks], 1),
        ],
        0,
    )
    high, low = split(half)
    done = mxu(tables[left, 0], high) + (mxu(tables[left, 0], low) + mxu(tables[left, 1], high))
    return [(done[:W, m * W : (m + 1) * W], done[W:, m * W : (m + 1) * W]) for m in range(count)]


STEP, STEP_BACK, DFT, DFT_BACK = (0, 1), (1, 0), (2, 3), (3, 2)


def chain(trans, trans_ready, probe, counts, tables, waves, grads, grad_done):
    fields = [(probe[0, m], probe[1, m]) for m in range(MODES)]
    for j in range(DEPTH):
        trans_ready(j)
        tr, ti = trans[j, 0], trans[j, 1]
        entering = []
        for m, (real, imag) in enumerate(fields):
            waves[j, m, 0] = real
            waves[j, m, 1] = imag
            entering.append((tr * real - ti * imag, tr * imag + ti * real))
        fields = transform(entering, tables, *(STEP if j < DEPTH - 1 else DFT))
    intensity = sum(real * real + imag * imag for real, imag in fields)
    residual = intensity - count_scale * counts[0].astype(jnp.float32)
    residual = (4.0 * loss_scale) * residual
    fields = [(residual * real, residual * imag) for real, imag in fields]
    for j in reversed(range(DEPTH)):
        fields = transform(fields, tables, *(STEP_BACK if j < DEPTH - 1 else DFT_BACK))
        tr, ti = trans[j, 0], trans[j, 1]
        leaving, phase_part, absorb_part = [], 0.0, 0.0
        for m, (real, imag) in enumerate(fields):
            real, imag = tr * real + ti * imag, tr * imag - ti * real
            wr, wi = waves[j, m, 0], waves[j, m, 1]
            phase_part = phase_part + (wr * imag - wi * real)
            absorb_part = absorb_part - (wr * real + wi * imag)
            leaving.append((real, imag))
        fields = leaving
        grads[j, :W] = phase_part
        grads[j, W:] = absorb_part
        grad_done(j)


def main_kernel(
    rows_hbm, cols_hbm, slots_hbm, phase, absorb, probe_hbm, counts_hbm, tables_hbm,
    out,
    rows, cols, slots, probe, counts, tables,
    padded, ext, a_recv, a_side, b_recv, b_sum, c_recv, window,
    trans, waves, grads, got,
    load_sems, s_send, s_recv, g_send, g_recv, t_send, t_recv, d_send, d_recv,
):
    me = lax.axis_index("tile")
    d = lax.axis_index("depth")
    barrier = pltpu.get_barrier_semaphore()
    greeted = tile_partners()
    loads = [
        pltpu.make_async_copy(source, target, load_sems.at[i])
        for i, (source, target) in enumerate(
            [(rows_hbm, rows), (cols_hbm, cols), (slots_hbm, slots)]
            + [
                (tile.at[0, 0, :, pl.ds(c * W, W)], padded.at[m, c + 1, pl.ds(W, TS)])
                for m, tile in enumerate((phase, absorb))
                for c in range(TS // W)
            ]
            + [(probe_hbm, probe), (counts_hbm, counts), (tables_hbm, tables)]
        )
    ]
    for load in loads[:3]:
        load.start()
    for m in range(2):
        for c in range(CHUNKS):
            if 1 <= c <= TS // W:
                padded[m, c, :W] = jnp.zeros((W, W), jnp.float32)
                padded[m, c, W + TS :] = jnp.zeros((W, W), jnp.float32)
            else:
                padded[m, c] = jnp.zeros((PADDED, W), jnp.float32)
    for load in loads[3:9]:
        load.start()
    for partner in greeted:
        pl.semaphore_signal(barrier, inc=1, device_id=partner, device_id_type=MESH)

    @pl.when(d == 0)
    def _():
        for k in range(1, DEPTH):
            pl.semaphore_signal(barrier, inc=1, device_id={"depth": k}, device_id_type=MESH)

    @pl.when(d != 0)
    def _():
        pl.semaphore_signal(barrier, inc=1, device_id={"depth": 0}, device_id_type=MESH)

    for load in loads[:9]:
        load.wait()
    top, left = tile_corner(slots, me)
    lane = lax.broadcasted_iota(jnp.int32, (W, W), 1)
    z, y = tile_place()

    def extract_one(dz, dy):
        p = turned(z, dz, NZ) * NY + turned(y, dy, NY)
        start = jnp.clip(rows[p] - top, -W, TS) + W
        column = jnp.clip(cols[p] - left, -W, TS) + W
        chunk = lax.shift_right_logical(column, 7)
        after = jnp.minimum(chunk + 1, CHUNKS - 1)
        shift = column - chunk * W
        back = lax.bitwise_and(W - shift, W - 1)
        for m in range(2):
            first = padded[m, chunk, pl.ds(start, W), :]
            second = padded[m, after, pl.ds(start, W), :]
            ext[spot(dz, dy), m * W : (m + 1) * W] = pltpu.roll(
                jnp.where(lane >= shift, first, second), back, 1
            )

    def extract(offset):
        for dy in range(NY):
            extract_one(offset, dy)

    def ready():
        pl.semaphore_wait(barrier, len(greeted) + jnp.where(d == 0, DEPTH - 1, 1))
        for load in loads[9:]:
            load.start()

    send = Sender(s_send, s_recv)
    scatter(extract, ready, ext, window, a_recv, a_side, b_recv, b_sum, c_recv, send)

    damping = jnp.exp(-window[W:])
    trans[d, 0] = damping * jnp.cos(window[:W])
    trans[d, 1] = damping * jnp.sin(window[:W])

    def trans_copy(j, send_slot):
        return pltpu.make_async_remote_copy(
            src_ref=trans.at[j],
            dst_ref=trans.at[j],
            send_sem=t_send.at[0],
            recv_sem=t_recv.at[j],
            device_id={"depth": send_slot},
            device_id_type=MESH,
        )

    def grad_copy(j):
        return pltpu.make_async_remote_copy(
            src_ref=grads.at[j],
            dst_ref=got,
            send_sem=d_send.at[j],
            recv_sem=d_recv.at[0],
            device_id={"depth": j},
            device_id_type=MESH,
        )

    @pl.when(d == 0)
    def _():
        for load in loads[9:]:
            load.wait()

        def trans_ready(j):
            if j > 0:
                trans_copy(j, 1).wait_recv()

        def grad_done(j):
            if j > 0:
                grad_copy(j).start()
            else:
                out[0] = grads[0]

        chain(trans, trans_ready, probe, counts, tables, waves, grads, grad_done)

    @pl.when(d != 0)
    def _():
        trans_copy(d, 0).start()
        for load in loads[9:]:
            load.wait()
        trans_copy(d, 0).wait_send()
        pltpu.make_async_remote_copy(
            src_ref=got,
            dst_ref=got,
            send_sem=d_send.at[0],
            recv_sem=d_recv.at[0],
            device_id={"depth": 0},
            device_id_type=MESH,
        ).wait_recv()
        out[0] = got[...]

    send_back = Sender(g_send, g_recv)
    gather(out, send_back)

    @pl.when(d == 0)
    def _():
        for j in range(1, DEPTH):
            grad_copy(j).wait_send()

    send.finish()
    send_back.finish()


def local(phase, absorb, probe, row_offsets, col_offsets, tile_slot, counts):
    f32 = jnp.float32
    mib = 1 << 20
    dma = pltpu.SemaphoreType.DMA
    tables = jnp.asarray(make_tables())
    gathered = pl.pallas_call(
        main_kernel,
        out_shape=jax.ShapeDtypeStruct((POS, BOTH, W), f32),
        in_specs=[HBM] * 8,
        out_specs=VMEM,
        scratch_shapes=[
            pltpu.SMEM((POS,), jnp.int32),
            pltpu.SMEM((POS,), jnp.int32),
            pltpu.SMEM((POS,), jnp.int32),
            pltpu.VMEM(probe.shape, f32),
            pltpu.VMEM(counts.shape, jnp.int32),
            pltpu.VMEM(tables.shape, jnp.bfloat16),
            pltpu.VMEM((2, CHUNKS, PADDED, W), f32),
            pltpu.VMEM((POS, BOTH, W), f32),
            pltpu.VMEM((28, ROWS_A, W), f32),
            pltpu.VMEM((2 * NY, ROWS_A, W), f32),
            pltpu.VMEM((24, ROWS_B, W), f32),
            pltpu.VMEM((NZ, ROWS_B, W), f32),
            pltpu.VMEM((8, ROWS_B, W), f32),
            pltpu.VMEM((BOTH, W), f32),
            pltpu.VMEM((DEPTH, 2, W, W), f32),
            pltpu.VMEM((DEPTH, MODES, 2, W, W), f32),
            pltpu.VMEM((DEPTH, BOTH, W), f32),
            pltpu.VMEM((BOTH, W), f32),
            dma((12,)),
            dma((SCATTER_COPIES,)),
            dma((SCATTER_COPIES,)),
            dma((GATHER_COPIES,)),
            dma((GATHER_COPIES,)),
            dma((1,)),
            dma((DEPTH,)),
            dma((DEPTH,)),
            dma((1,)),
        ],
        compiler_params=pltpu.CompilerParams(
            collective_id=0, has_side_effects=True, vmem_limit_bytes=60 * mib
        ),
        name="main",
    )(row_offsets, col_offsets, tile_slot, phase, absorb, probe, counts, tables)
    return pl.pallas_call(
        deposit_kernel,
        out_shape=(jax.ShapeDtypeStruct((1, 1, TS, TS), f32),) * 2,
        in_specs=[SMEM, SMEM, SMEM, ANY],
        out_specs=(VMEM, VMEM),
        scratch_shapes=[
            pltpu.VMEM((2, TS // W + 2, PADDED, W), f32),
            pltpu.VMEM((POS, BOTH, W), f32),
            dma((POS,)),
        ],
        compiler_params=pltpu.CompilerParams(vmem_limit_bytes=60 * mib),
        name="deposit",
    )(row_offsets, col_offsets, tile_slot, gathered)


def solution(mesh):
    in_specs = (
        P("depth", "tile", None, None),
        P("depth", "tile", None, None),
        P(),
        P(),
        P(),
        P(),
        P("tile", None, None),
    )
    out_specs = (P("depth", "tile", None, None), P("depth", "tile", None, None))
    return jax.shard_map(local, mesh=mesh, in_specs=in_specs, out_specs=out_specs, check_vma=False)
```

```python
import functools
import math

import numpy as np
import jax
import jax.numpy as jnp
from jax import lax
from jax.experimental import pallas as pl
from jax.experimental.pallas import tpu as pltpu
from jax.sharding import PartitionSpec as P

W = 128
MODES = 4
TS = 384
GY = 4
POS = 32
NZ = 8
NY = 4
DEPTH = 8
BOTH = 2 * W
PIXELS = 48
ROWS_A = 2 * PIXELS
ROWS_B = BOTH - ROWS_A
HALF_B = ROWS_B // 2
REST = W - PIXELS
BANDS = (
    (slice(0, PIXELS), 0, slice(0, PIXELS)),
    (slice(PIXELS, ROWS_A), 1, slice(0, PIXELS)),
    (slice(ROWS_A, ROWS_A + REST), 0, slice(PIXELS, W)),
    (slice(ROWS_A + REST, BOTH), 1, slice(PIXELS, W)),
)
CHUNKS = TS // W + 2
PADDED = TS + 2 * W

count_scale = 0.0078125
loss_scale = 0.03125
fresnel_strength = 40.0

VMEM = pl.BlockSpec(memory_space=pltpu.VMEM)
SMEM = pl.BlockSpec(memory_space=pltpu.SMEM)
HBM = pl.BlockSpec(memory_space=pltpu.HBM)
ANY = pl.BlockSpec(memory_space=pl.ANY)
MESH = pl.DeviceIdType.MESH


def make_tables():
    index = np.arange(W)
    angle = 2.0 * np.pi * ((index[:, None] * index[None, :]) % W) / W
    dft = np.exp(-1j * angle) / math.sqrt(W)
    signed = ((index + W // 2) % W - W // 2) / W
    chirp = np.exp(-1j * fresnel_strength * signed**2)
    step = np.conj(dft) @ (chirp[:, None] * dft)
    tables = []
    for g in (step, dft):
        right = np.block([[g.real, g.imag], [-g.imag, g.real]])
        for table in (right, right.T):
            table = table.astype(np.float32)
            high = table.astype(jnp.bfloat16)
            low = (table - high.astype(np.float32)).astype(jnp.bfloat16)
            tables.append(np.stack([high, low]))
    return np.stack(tables)


def tile_corner(slots, me):
    def look(i, place):
        return jnp.where(slots[i] == me, i, place)

    place = lax.fori_loop(0, POS, look, jnp.int32(0))
    row = lax.shift_right_logical(place, 2)
    return row * TS, (place - row * GY) * TS


def overlap(rows, cols, p, top, left):
    dr = rows[p] - top
    dc = cols[p] - left
    return dr, dc, (dr > -W) & (dr < TS) & (dc > -W) & (dc < TS)


def deposit_kernel(rows, cols, slots, grads, phase_out, absorb_out, acc, held, sems):
    me = lax.axis_index("tile")
    top, left = tile_corner(slots, me)

    z, y = tile_place()

    def fetch(p):
        row = lax.shift_right_logical(p, 2)
        place = turned(row, -z, NZ) * NY + turned(p - row * NY, -y, NY)
        return pltpu.make_async_copy(grads.at[place], held.at[p], sems.at[p])

    def begin(p, carry):
        dr, dc, touches = overlap(rows, cols, p, top, left)

        @pl.when(touches)
        def _():
            fetch(p).start()

        return carry

    lax.fori_loop(0, POS, begin, 0)
    acc[...] = jnp.zeros_like(acc)
    lane = lax.broadcasted_iota(jnp.int32, (W, W), 1)

    def one(p, carry):
        dr, dc, touches = overlap(rows, cols, p, top, left)

        @pl.when(touches)
        def _():
            fetch(p).wait()
            start = dr + W
            chunk = lax.shift_right_logical(dc + W, 7)
            shift = dc + W - chunk * W
            for m in range(2):
                pieces = [held[p, rows_in] for rows_in, kind, _ in BANDS if kind == m]
                moved = pltpu.roll(jnp.concatenate(pieces, 0), shift, 1)
                acc[m, chunk, pl.ds(start, W), :] += jnp.where(lane >= shift, moved, 0.0)
                acc[m, chunk + 1, pl.ds(start, W), :] += jnp.where(lane < shift, moved, 0.0)

        return carry

    lax.fori_loop(0, POS, one, 0)
    for m, target in enumerate((phase_out, absorb_out)):
        for c in range(TS // W):
            target[0, 0, :, c * W : (c + 1) * W] = acc[m, c + 1, W : W + TS, :]


def tile_place():
    me = lax.axis_index("tile")
    z = me // NY
    return z, me - z * NY


def turned(value, step, count):
    return lax.rem(value + step + count, count)


def z_device(way):
    z, y = tile_place()
    return {"tile": turned(z, way, NZ) * NY + y}


def y_device(step):
    z, y = tile_place()
    return {"tile": z * NY + turned(y, step, NY)}


def tile_partners():
    return [z_device(k) for k in (1, -1, 2, -2)] + [y_device(k) for k in range(1, NY)]


class Sender:
    def __init__(self, send_sems, recv_sems):
        self.send_sems, self.recv_sems = send_sems, recv_sems
        self.started = []

    def copy(self, source, target, device):
        n = len(self.started)
        copy = pltpu.make_async_remote_copy(
            src_ref=source,
            dst_ref=target,
            send_sem=self.send_sems.at[n],
            recv_sem=self.recv_sems.at[n],
            device_id=device,
            device_id_type=MESH,
        )
        copy.start()
        self.started.append(copy)
        return copy

    def finish(self):
        for copy in self.started:
            copy.wait_send()


HOPS4 = ((0, 1), (1, 1), (2, -1), (3, -1))
HOPS3 = ((2, 1), (3, 1), (0, -1), (1, -1))
SCATTER_COPIES = 28 + 3 + 24 + 8
GATHER_COPIES = 28 + 3 + 24 + 8
FAR_FIRST = (4, 3, -3, 2, -2, 1, -1, 0)
PART_A = pl.ds(0, ROWS_A)
PART_B = pl.ds(ROWS_A, ROWS_B)
ALL_B = pl.ds(0, ROWS_B)


def half_of(way):
    return 0 if way == 1 else HALF_B


def spot(dz, dy):
    return (dz % NZ) * NY + dy % NY


def scatter(extract, ready, done_a, done_b, ext, a_recv, a_side, b_recv, b_sum, c_recv, send):
    a_last, b_last, c_last = {}, {}, {}
    a_slots, b_slots = iter(range(28)), iter(range(24))

    def a_step(streams, length, s):
        for stream, way in streams:
            dest = spot(way * (length - s), stream)
            if s > 0:
                copy, slot = a_last[stream, way]
                copy.wait_recv()
                a_recv[slot] += ext[dest, PART_A]
                source = a_recv.at[slot]
            else:
                source = ext.at[dest, PART_A]
            slot = next(a_slots)
            a_last[stream, way] = (send.copy(source, a_recv.at[slot], z_device(way)), slot)

    def b_send(offset, way, source):
        slot = next(b_slots)
        b_last[offset, way] = (send.copy(source, b_recv.at[slot], y_device(way)), slot)

    def b_far(offset):
        way = 1 if offset % 2 == 0 else -1
        b_send(offset, way, ext.at[spot(offset, 2), PART_B])
        b_send(offset, -way, ext.at[spot(offset, -way), PART_B])

    def b_near(offset):
        way = 1 if offset % 2 == 0 else -1
        copy, slot = b_last[offset, way]
        copy.wait_recv()
        b_recv[slot] += ext[spot(offset, way), PART_B]
        b_send(offset, way, b_recv.at[slot])

    def b_total(offset):
        total = ext[spot(offset, 0), PART_B]
        for way in (1, -1):
            copy, slot = b_last[offset, way]
            copy.wait_recv()
            total = total + b_recv[slot]
        b_sum[offset % NZ] = total

    def c_send(away, way):
        slot = 2 * (away - 1) + (way < 0)
        part = pl.ds(half_of(way), HALF_B) if away == 4 else ALL_B
        source = b_sum.at[way * away % NZ, part]
        if away < 4:
            if (away + 1, way) in c_last:
                copy, held = c_last[away + 1, way]
                copy.wait_recv()
                part_held = pl.ds(half_of(way), HALF_B) if away == 3 else ALL_B
                b_sum[way * away % NZ, part_held] += c_recv[held, part_held]
        target = c_recv.at[slot, part]
        c_last[away, way] = (send.copy(source, target, z_device(way)), slot)

    extract(4)
    ready()
    a_step(HOPS4, 4, 0)
    b_far(4)
    extract(3)
    a_step(HOPS3[:2], 3, 0)
    b_far(3)
    extract(-3)
    a_step(HOPS3[2:], 3, 0)
    b_near(4)
    b_far(-3)
    extract(2)
    extract(-2)
    a_step(HOPS4, 4, 1)
    b_near(3)
    b_far(2)
    extract(1)
    extract(-1)
    b_total(4)
    c_send(4, 1)
    c_send(4, -1)
    a_step(HOPS3, 3, 1)
    b_near(-3)
    b_far(-2)
    extract(0)
    b_total(3)
    c_send(3, 1)
    a_step(HOPS4, 4, 2)
    b_near(2)
    b_far(1)
    b_total(-3)
    c_send(3, -1)
    a_step(HOPS3, 3, 2)
    b_near(-2)
    b_far(-1)
    b_total(2)
    c_send(2, 1)
    a_step(HOPS4, 4, 3)
    b_near(1)
    b_far(0)
    b_total(-2)
    c_send(2, -1)
    for stream in (1, 3, 2, 0):
        total = ext[spot(0, stream), PART_A]
        for way in (1, -1):
            copy, slot = a_last[stream, way]
            copy.wait_recv()
            total = total + a_recv[slot]
        a_side[stream] = total
        if stream > 0:
            a_last[stream] = send.copy(a_side.at[stream], a_side.at[NY + stream], y_device(stream))
    b_near(-1)
    b_total(1)
    c_send(1, 1)
    b_near(0)
    b_total(-1)
    c_send(1, -1)
    total = a_side[0]
    for stream in (1, 3, 2):
        a_last[stream].wait_recv()
        total = total + a_side[NY + stream]
    done_a(total)
    b_total(0)
    total = b_sum[0]
    for way in (1, -1):
        copy, slot = c_last[1, way]
        copy.wait_recv()
        total = total + c_recv[slot]
    done_b(total)


def gather(held, keep, send):
    a_last, b_last, c_last = {}, {}, {}

    def z_copy(dz, dy, part, way):
        source, target = held.at[spot(dz, dy), part], held.at[spot(dz - way, dy), part]
        return send.copy(source, target, z_device(way))

    def y_copy(dz, dy, part, way):
        source, target = held.at[spot(dz, dy), part], held.at[spot(dz, dy - way), part]
        return send.copy(source, target, y_device(way))

    def a_first():
        for step in (1, 3, 2):
            a_last[step] = y_copy(0, 0, PART_A, step)

    def a_step(s, streams):
        if s == 0:
            for stream in streams:
                if stream > 0:
                    a_last[stream].wait_recv()
                    keep(0, -stream, PART_A)
        for found, length in ((HOPS4, 4), (HOPS3, 3)):
            for stream, way in found:
                if s > length or stream not in streams:
                    continue
                if s > 0:
                    a_last[stream, way].wait_recv()
                    keep(-way * s, -stream, PART_A)
                if s < length:
                    a_last[stream, way] = z_copy(-way * s, -stream, PART_A, way)

    def c_send(away, way):
        part = pl.ds(ROWS_A + half_of(way), HALF_B) if away == 4 else PART_B
        if away > 1:
            c_last[away - 1, way].wait_recv()
        c_last[away, way] = z_copy(-way * (away - 1), 0, part, way)

    def b_first(offset):
        for way in (1, -1):
            b_last[offset, way] = y_copy(offset, 0, PART_B, way)
        if offset != 0:
            keep(offset, 0, PART_B)

    def b_second(offset):
        way = 1 if offset % 2 == 0 else -1
        b_last[offset, way].wait_recv()
        b_last[offset, 2] = y_copy(offset, -way, PART_B, way)
        keep(offset, -way, PART_B)

    def b_last_two(offset):
        way = 1 if offset % 2 == 0 else -1
        b_last[offset, -way].wait_recv()
        keep(offset, way, PART_B)
        b_last[offset, 2].wait_recv()
        keep(offset, 2, PART_B)

    c_send(1, 1)
    c_send(1, -1)
    a_first()
    b_first(0)
    a_step(0, (0,))
    for way in (1, -1):
        c_send(2, way)
        b_first(-way)
    keep(0, 0, pl.ds(0, BOTH))
    a_step(0, (1,))
    a_step(0, (3,))
    b_second(0)
    a_step(0, (2,))
    for way in (1, -1):
        c_send(3, way)
        b_first(-2 * way)
    a_step(1, (0,))
    b_second(1)
    b_second(-1)
    a_step(1, (1,))
    a_step(1, (3,))
    for way in (1, -1):
        c_send(4, way)
        b_first(-3 * way)
    a_step(1, (2,))
    b_last_two(0)
    b_second(2)
    b_second(-2)
    a_step(2, (0,))
    a_step(2, (1,))
    a_step(2, (3,))
    for way in (1, -1):
        c_last[4, way].wait_recv()
    b_first(4)
    b_last_two(1)
    b_last_two(-1)
    a_step(2, (2,))
    b_second(3)
    b_second(-3)
    a_step(3, (0,))
    b_last_two(2)
    b_last_two(-2)
    a_step(3, (1, 3, 2))
    b_second(4)
    a_step(4, (0, 1, 3, 2))
    b_last_two(3)
    b_last_two(-3)
    b_last_two(4)


def split(value):
    high = value.astype(jnp.bfloat16)
    low = (value - high.astype(jnp.float32)).astype(jnp.bfloat16)
    return high, low


def mxu(a, b):
    return jnp.dot(a, b, preferred_element_type=jnp.float32)


def transform(fields, tables, right, left):
    halves = []
    for field in fields:
        high, low = split(jnp.concatenate(field, 1))
        halves.append(
            mxu(high, tables[right, 0])
            + (mxu(low, tables[right, 0]) + mxu(high, tables[right, 1]))
        )
    done = []
    for half in halves:
        high, low = split(jnp.concatenate([half[:, :W], half[:, W:]], 0))
        both = mxu(tables[left, 0], jnp.concatenate([high, low], 1))
        whole = both[:, :W] + (both[:, W:] + mxu(tables[left, 1], high))
        done.append((whole[:W], whole[W:]))
    return done


STEP, STEP_BACK, DFT, DFT_BACK = (0, 1), (1, 0), (2, 3), (3, 2)


def chain(trans, trans_ready, probe, counts, tables, waves, grads, grad_done):
    fields = [(probe[0, m], probe[1, m]) for m in range(MODES)]
    for j in range(DEPTH):
        trans_ready(j)
        tr, ti = trans[j, 0], trans[j, 1]
        entering = []
        for m, (real, imag) in enumerate(fields):
            waves[j, m, 0] = real
            waves[j, m, 1] = imag
            entering.append((tr * real - ti * imag, tr * imag + ti * real))
        fields = transform(entering, tables, *(STEP if j < DEPTH - 1 else DFT))
    intensity = sum(real * real + imag * imag for real, imag in fields)
    residual = intensity - count_scale * counts[0].astype(jnp.float32)
    residual = (4.0 * loss_scale) * residual
    fields = [(residual * real, residual * imag) for real, imag in fields]
    for j in reversed(range(DEPTH)):
        fields = transform(fields, tables, *(STEP_BACK if j < DEPTH - 1 else DFT_BACK))
        tr, ti = trans[j, 0], trans[j, 1]
        leaving, phase_part, absorb_part = [], 0.0, 0.0
        for m, (real, imag) in enumerate(fields):
            real, imag = tr * real + ti * imag, tr * imag - ti * real
            wr, wi = waves[j, m, 0], waves[j, m, 1]
            phase_part = phase_part + (wr * imag - wi * real)
            absorb_part = absorb_part - (wr * real + wi * imag)
            leaving.append((real, imag))
        fields = leaving
        for rows_in, kind, rows_of in BANDS:
            grads[j, rows_in] = (phase_part, absorb_part)[kind][rows_of]
        grad_done(j)


def main_kernel(
    rows_hbm, cols_hbm, slots_hbm, phase, absorb, probe_hbm, counts_hbm, tables_hbm,
    out,
    rows, cols, slots, probe, counts, tables,
    padded, ext, a_recv, a_side, b_recv, b_sum, c_recv, held,
    trans, waves, grads, got,
    load_sems, s_send, s_recv, g_send, g_recv, t_send, t_recv, d_send, d_recv, keep_sems,
):
    me = lax.axis_index("tile")
    d = lax.axis_index("depth")
    barrier = pltpu.get_barrier_semaphore()
    greeted = tile_partners()
    loads = [
        pltpu.make_async_copy(source, target, load_sems.at[i])
        for i, (source, target) in enumerate(
            [(rows_hbm, rows), (cols_hbm, cols), (slots_hbm, slots)]
            + [
                (tile.at[0, 0, :, pl.ds(c * W, W)], padded.at[m, c + 1, pl.ds(W, TS)])
                for m, tile in enumerate((phase, absorb))
                for c in range(TS // W)
            ]
            + [(probe_hbm, probe), (counts_hbm, counts), (tables_hbm, tables)]
        )
    ]
    for load in loads[:3]:
        load.start()
    for m in range(2):
        for c in range(CHUNKS):
            if 1 <= c <= TS // W:
                padded[m, c, :W] = jnp.zeros((W, W), jnp.float32)
                padded[m, c, W + TS :] = jnp.zeros((W, W), jnp.float32)
            else:
                padded[m, c] = jnp.zeros((PADDED, W), jnp.float32)
    for load in loads[3:9]:
        load.start()
    for partner in greeted:
        pl.semaphore_signal(barrier, inc=1, device_id=partner, device_id_type=MESH)

    @pl.when(d == 0)
    def _():
        for k in range(1, DEPTH):
            pl.semaphore_signal(barrier, inc=1, device_id={"depth": k}, device_id_type=MESH)

    @pl.when(d != 0)
    def _():
        pl.semaphore_signal(barrier, inc=1, device_id={"depth": 0}, device_id_type=MESH)

    for load in loads[:9]:
        load.wait()
    top, left = tile_corner(slots, me)
    lane = lax.broadcasted_iota(jnp.int32, (W, W), 1)
    z, y = tile_place()

    def extract_one(dz, dy):
        p = turned(z, dz, NZ) * NY + turned(y, dy, NY)
        start = jnp.clip(rows[p] - top, -W, TS) + W
        column = jnp.clip(cols[p] - left, -W, TS) + W
        chunk = lax.shift_right_logical(column, 7)
        after = jnp.minimum(chunk + 1, CHUNKS - 1)
        shift = column - chunk * W
        back = lax.bitwise_and(W - shift, W - 1)
        for m in range(2):
            first = padded[m, chunk, pl.ds(start, W), :]
            second = padded[m, after, pl.ds(start, W), :]
            moved = pltpu.roll(jnp.where(lane >= shift, first, second), back, 1)
            for rows_in, kind, rows_of in BANDS:
                if kind == m:
                    ext[spot(dz, dy), rows_in] = moved[rows_of]

    def extract(offset):
        for dy in range(NY):
            extract_one(offset, dy)

    def ready():
        pl.semaphore_wait(barrier, len(greeted) + jnp.where(d == 0, DEPTH - 1, 1))
        for load in loads[9:]:
            load.start()

    send = Sender(s_send, s_recv)

    def trans_copy(j, part):
        rows_of = pl.ds(0, PIXELS) if part == 0 else pl.ds(PIXELS, REST)
        return pltpu.make_async_remote_copy(
            src_ref=trans.at[j, :, rows_of],
            dst_ref=trans.at[j, :, rows_of],
            send_sem=t_send.at[part],
            recv_sem=t_recv.at[part, j],
            device_id={"depth": 0},
            device_id_type=MESH,
        )

    def done(part):
        def put(total):
            rows_of = slice(0, PIXELS) if part == 0 else slice(PIXELS, W)
            count = total.shape[0] // 2
            damping = jnp.exp(-total[count:])
            trans[d, 0, rows_of] = damping * jnp.cos(total[:count])
            trans[d, 1, rows_of] = damping * jnp.sin(total[:count])

            @pl.when(d != 0)
            def _():
                trans_copy(d, part).start()

        return put

    scatter(
        extract, ready, done(0), done(1), ext, a_recv, a_side, b_recv, b_sum, c_recv, send
    )

    def grad_copy(j):
        return pltpu.make_async_remote_copy(
            src_ref=grads.at[j],
            dst_ref=got,
            send_sem=d_send.at[j],
            recv_sem=d_recv.at[0],
            device_id={"depth": j},
            device_id_type=MESH,
        )

    @pl.when(d == 0)
    def _():
        for load in loads[9:]:
            load.wait()

        def trans_ready(j):
            if j > 0:
                for part in range(2):
                    pltpu.make_async_remote_copy(
                        src_ref=trans.at[j, :, pl.ds(part * PIXELS, (PIXELS, REST)[part])],
                        dst_ref=trans.at[j, :, pl.ds(part * PIXELS, (PIXELS, REST)[part])],
                        send_sem=t_send.at[part],
                        recv_sem=t_recv.at[part, j],
                        device_id={"depth": 1},
                        device_id_type=MESH,
                    ).wait_recv()

        def grad_done(j):
            if j > 0:
                grad_copy(j).start()
            else:
                held[0] = grads[0]

        chain(trans, trans_ready, probe, counts, tables, waves, grads, grad_done)

    @pl.when(d != 0)
    def _():
        for load in loads[9:]:
            load.wait()
        for part in range(2):
            trans_copy(d, part).wait_send()
        pltpu.make_async_remote_copy(
            src_ref=got,
            dst_ref=got,
            send_sem=d_send.at[0],
            recv_sem=d_recv.at[0],
            device_id={"depth": 0},
            device_id_type=MESH,
        ).wait_recv()
        held[0] = got[...]

    send_back = Sender(g_send, g_recv)
    kept = []

    def keep(dz, dy, part):
        place = spot(dz, dy)
        copy = pltpu.make_async_copy(
            held.at[place, part], out.at[place, part], keep_sems.at[len(kept)]
        )
        copy.start()
        kept.append(copy)

    gather(held, keep, send_back)

    @pl.when(d == 0)
    def _():
        for j in range(1, DEPTH):
            grad_copy(j).wait_send()

    send.finish()
    send_back.finish()
    for copy in kept:
        copy.wait()


def local(phase, absorb, probe, row_offsets, col_offsets, tile_slot, counts):
    f32 = jnp.float32
    mib = 1 << 20
    dma = pltpu.SemaphoreType.DMA
    tables = jnp.asarray(make_tables())
    gathered = pl.pallas_call(
        main_kernel,
        out_shape=jax.ShapeDtypeStruct((POS, BOTH, W), f32),
        in_specs=[HBM] * 8,
        out_specs=HBM,
        scratch_shapes=[
            pltpu.SMEM((POS,), jnp.int32),
            pltpu.SMEM((POS,), jnp.int32),
            pltpu.SMEM((POS,), jnp.int32),
            pltpu.VMEM(probe.shape, f32),
            pltpu.VMEM(counts.shape, jnp.int32),
            pltpu.VMEM(tables.shape, jnp.bfloat16),
            pltpu.VMEM((2, CHUNKS, PADDED, W), f32),
            pltpu.VMEM((POS, BOTH, W), f32),
            pltpu.VMEM((28, ROWS_A, W), f32),
            pltpu.VMEM((2 * NY, ROWS_A, W), f32),
            pltpu.VMEM((24, ROWS_B, W), f32),
            pltpu.VMEM((NZ, ROWS_B, W), f32),
            pltpu.VMEM((8, ROWS_B, W), f32),
            pltpu.VMEM((POS, BOTH, W), f32),
            pltpu.VMEM((DEPTH, 2, W, W), f32),
            pltpu.VMEM((DEPTH, MODES, 2, W, W), f32),
            pltpu.VMEM((DEPTH, BOTH, W), f32),
            pltpu.VMEM((BOTH, W), f32),
            dma((12,)),
            dma((SCATTER_COPIES,)),
            dma((SCATTER_COPIES,)),
            dma((GATHER_COPIES,)),
            dma((GATHER_COPIES,)),
            dma((2,)),
            dma((2, DEPTH)),
            dma((DEPTH,)),
            dma((1,)),
            dma((2 * POS,)),
        ],
        compiler_params=pltpu.CompilerParams(
            collective_id=0, has_side_effects=True, vmem_limit_bytes=60 * mib
        ),
        name="main",
    )(row_offsets, col_offsets, tile_slot, phase, absorb, probe, counts, tables)
    return pl.pallas_call(
        deposit_kernel,
        out_shape=(jax.ShapeDtypeStruct((1, 1, TS, TS), f32),) * 2,
        in_specs=[SMEM, SMEM, SMEM, ANY],
        out_specs=(VMEM, VMEM),
        scratch_shapes=[
            pltpu.VMEM((2, TS // W + 2, PADDED, W), f32),
            pltpu.VMEM((POS, BOTH, W), f32),
            dma((POS,)),
        ],
        compiler_params=pltpu.CompilerParams(vmem_limit_bytes=60 * mib),
        name="deposit",
    )(row_offsets, col_offsets, tile_slot, gathered)


def solution(mesh):
    in_specs = (
        P("depth", "tile", None, None),
        P("depth", "tile", None, None),
        P(),
        P(),
        P(),
        P(),
        P("tile", None, None),
    )
    out_specs = (P("depth", "tile", None, None), P("depth", "tile", None, None))
    return jax.shard_map(local, mesh=mesh, in_specs=in_specs, out_specs=out_specs, check_vma=False)
```

```python
import functools
import math

import numpy as np
import jax
import jax.numpy as jnp
from jax import lax
from jax.experimental import pallas as pl
from jax.experimental.pallas import tpu as pltpu
from jax.sharding import PartitionSpec as P

W = 128
MODES = 4
TS = 384
GY = 4
POS = 32
NZ = 8
NY = 4
DEPTH = 8
BOTH = 2 * W
PIXELS = 56
ROWS_A = 2 * PIXELS
ROWS_B = BOTH - ROWS_A
HALF_B = ROWS_B // 2
REST = W - PIXELS
BANDS = (
    (slice(0, PIXELS), 0, slice(0, PIXELS)),
    (slice(PIXELS, ROWS_A), 1, slice(0, PIXELS)),
    (slice(ROWS_A, ROWS_A + REST), 0, slice(PIXELS, W)),
    (slice(ROWS_A + REST, BOTH), 1, slice(PIXELS, W)),
)
CHUNKS = TS // W + 2
PADDED = TS + 2 * W

count_scale = 0.0078125
loss_scale = 0.03125
fresnel_strength = 40.0

VMEM = pl.BlockSpec(memory_space=pltpu.VMEM)
SMEM = pl.BlockSpec(memory_space=pltpu.SMEM)
HBM = pl.BlockSpec(memory_space=pltpu.HBM)
ANY = pl.BlockSpec(memory_space=pl.ANY)
MESH = pl.DeviceIdType.MESH


def make_tables():
    index = np.arange(W)
    angle = 2.0 * np.pi * ((index[:, None] * index[None, :]) % W) / W
    dft = np.exp(-1j * angle) / math.sqrt(W)
    signed = ((index + W // 2) % W - W // 2) / W
    chirp = np.exp(-1j * fresnel_strength * signed**2)
    step = np.conj(dft) @ (chirp[:, None] * dft)
    tables = []
    for g in (step, dft):
        right = np.block([[g.real, g.imag], [-g.imag, g.real]])
        for table in (right, right.T):
            table = table.astype(np.float32)
            high = table.astype(jnp.bfloat16)
            low = (table - high.astype(np.float32)).astype(jnp.bfloat16)
            tables.append(np.stack([high, low]))
    return np.stack(tables)


def tile_corner(slots, me):
    def look(i, place):
        return jnp.where(slots[i] == me, i, place)

    place = lax.fori_loop(0, POS, look, jnp.int32(0))
    row = lax.shift_right_logical(place, 2)
    return row * TS, (place - row * GY) * TS


def overlap(rows, cols, p, top, left):
    dr = rows[p] - top
    dc = cols[p] - left
    return dr, dc, (dr > -W) & (dr < TS) & (dc > -W) & (dc < TS)


def deposit_kernel(rows, cols, slots, grads, phase_out, absorb_out, acc, held, sems):
    me = lax.axis_index("tile")
    top, left = tile_corner(slots, me)

    z, y = tile_place()

    def fetch(p):
        row = lax.shift_right_logical(p, 2)
        place = turned(row, -z, NZ) * NY + turned(p - row * NY, -y, NY)
        return pltpu.make_async_copy(grads.at[place], held.at[p], sems.at[p])

    def begin(p, carry):
        dr, dc, touches = overlap(rows, cols, p, top, left)

        @pl.when(touches)
        def _():
            fetch(p).start()

        return carry

    lax.fori_loop(0, POS, begin, 0)
    acc[...] = jnp.zeros_like(acc)
    lane = lax.broadcasted_iota(jnp.int32, (W, W), 1)

    def one(p, carry):
        dr, dc, touches = overlap(rows, cols, p, top, left)

        @pl.when(touches)
        def _():
            fetch(p).wait()
            start = dr + W
            chunk = lax.shift_right_logical(dc + W, 7)
            shift = dc + W - chunk * W
            for m in range(2):
                pieces = [held[p, rows_in] for rows_in, kind, _ in BANDS if kind == m]
                moved = pltpu.roll(jnp.concatenate(pieces, 0), shift, 1)
                acc[m, chunk, pl.ds(start, W), :] += jnp.where(lane >= shift, moved, 0.0)
                acc[m, chunk + 1, pl.ds(start, W), :] += jnp.where(lane < shift, moved, 0.0)

        return carry

    lax.fori_loop(0, POS, one, 0)
    for m, target in enumerate((phase_out, absorb_out)):
        for c in range(TS // W):
            target[0, 0, :, c * W : (c + 1) * W] = acc[m, c + 1, W : W + TS, :]


def tile_place():
    me = lax.axis_index("tile")
    z = me // NY
    return z, me - z * NY


def turned(value, step, count):
    return lax.rem(value + step + count, count)


def z_device(way):
    z, y = tile_place()
    return {"tile": turned(z, way, NZ) * NY + y}


def y_device(step):
    z, y = tile_place()
    return {"tile": z * NY + turned(y, step, NY)}


def tile_partners():
    return [z_device(k) for k in (1, -1, 2, -2)] + [y_device(k) for k in range(1, NY)]


class Sender:
    def __init__(self, send_sems, recv_sems):
        self.send_sems, self.recv_sems = send_sems, recv_sems
        self.started = []

    def copy(self, source, target, device):
        n = len(self.started)
        copy = pltpu.make_async_remote_copy(
            src_ref=source,
            dst_ref=target,
            send_sem=self.send_sems.at[n],
            recv_sem=self.recv_sems.at[n],
            device_id=device,
            device_id_type=MESH,
        )
        copy.start()
        self.started.append(copy)
        return copy

    def finish(self):
        for copy in self.started:
            copy.wait_send()


HOPS = {
    (0, 1): 4, (1, 1): 4, (2, -1): 4, (3, -1): 4, (2, 1): 3, (3, 1): 3, (0, -1): 3, (1, -1): 3,
}
SCATTER_ORDER = (
    ("cut", 4, 1), ("cut", 4, 3), ("cut", 4, 2), ("far", 4), ("cut", 3, 2), ("a", 1, 1, 0),
    ("a", 3, -1, 0), ("cut", -1, 2), ("a", 2, 1, 0), ("cut", -3, 0), ("cut", -3, 2),
    ("cut", 3, 1), ("a", 2, -1, 0), ("cut", -2, 3), ("cut", -3, 1), ("far", 3), ("cut", 3, 3),
    ("cut", -2, 1), ("far", -3), ("cut", 4, 0), ("cut", -1, 0), ("a", 3, 1, 0), ("cut", -1, 3),
    ("a", 1, -1, 0), ("cut", 3, 0), ("cut", 1, 1), ("a", 0, 1, 0), ("cut", 0, 2), ("cut", -2, 0),
    ("a", 0, -1, 0), ("cut", -2, 2), ("near", 4), ("cut", -3, 3), ("cut", 2, 0), ("a", 1, 1, 1),
    ("cut", 0, 1), ("cut", 2, 1), ("cut", 1, 2), ("far", -2), ("a", 2, -1, 1), ("cut", 2, 3),
    ("cut", 0, 3), ("a", 1, -1, 1), ("near", -3), ("a", 3, 1, 1), ("a", 3, -1, 1), ("cut", 2, 2),
    ("a", 0, -1, 1), ("a", 0, 1, 1), ("a", 1, 1, 2), ("far", 2), ("sum", 4), ("near", 3),
    ("c", 4, 1), ("a", 2, 1, 1), ("near", -2), ("cut", -1, 1), ("a", 2, -1, 2), ("c", 4, -1),
    ("far", -1), ("sum", -3), ("near", 2), ("a", 3, -1, 2), ("cut", 1, 3), ("a", 3, 1, 2),
    ("cut", 0, 0), ("a", 1, -1, 2), ("far", 0), ("a", 1, 1, 3), ("c", 3, -1), ("sum", 3),
    ("c", 3, 1), ("far", 1), ("a", 3, -1, 3), ("a", 2, 1, 2), ("near", -1), ("a", 2, -1, 3),
    ("side", 1), ("sum", -2), ("a", 0, 1, 2), ("c", 2, -1), ("sum", 2), ("near", 1), ("c", 2, 1),
    ("near", 0), ("side", 3), ("a", 0, -1, 2), ("sum", -1), ("cut", 1, 0), ("a", 0, 1, 3),
    ("side", 2), ("sum", 1), ("c", 1, -1), ("c", 1, 1), ("sum", 0), ("side", 0), ("done_a",),
    ("done_b",),
)
GATHER_ORDER = (
    ("c", 1, 1), ("c", 1, -1), ("a_first",), ("first", 0), ("a", 0, -1, 0), ("a", 0, 1, 0),
    ("c", 2, 1), ("first", -1), ("c", 2, -1), ("a", 2, 1, 0), ("a", 0, -1, 1), ("a", 3, -1, 0),
    ("a", 0, 1, 1), ("first", -2), ("second", 0), ("c", 3, 1), ("a", 2, -1, 0), ("first", 2),
    ("first", 1), ("a", 1, 1, 0), ("c", 3, -1), ("second", -1), ("a", 3, -1, 1), ("a", 2, 1, 1),
    ("a", 3, 1, 0), ("a", 2, -1, 1), ("a", 1, -1, 0), ("a", 0, 1, 2), ("first", -3),
    ("a", 1, 1, 1), ("a", 3, -1, 2), ("c", 4, 1), ("first", 3), ("c", 4, -1), ("a", 3, 1, 1),
    ("a", 2, -1, 2), ("second", 1), ("second", 2), ("a", 2, 1, 2), ("end", -1), ("a", 1, -1, 1),
    ("a", 1, 1, 2), ("first", 4), ("a", 0, -1, 2), ("second", 3), ("a", 3, 1, 2), ("a", 0, 1, 3),
    ("second", -2), ("a", 3, -1, 3), ("a", 1, -1, 2), ("end", 2), ("end", 0), ("end", 1),
    ("second", -3), ("a", 2, -1, 3), ("a", 1, 1, 3), ("second", 4), ("a_end", 0, 1), ("end", 3),
    ("end", -2), ("a_end", 0, -1), ("a_end", 3, 1), ("a_end", 3, -1), ("end", -3),
    ("a_end", 1, -1), ("a_end", 2, 1), ("a_end", 1, 1), ("end", 4), ("a_end", 2, -1),
)
SCATTER_COPIES = 28 + 3 + 24 + 8
GATHER_COPIES = 28 + 3 + 24 + 8
PART_A = pl.ds(0, ROWS_A)
PART_B = pl.ds(ROWS_A, ROWS_B)
ALL_B = pl.ds(0, ROWS_B)


def half_of(way):
    return 0 if way == 1 else HALF_B


def spot(dz, dy):
    return (dz % NZ) * NY + dy % NY


class Arrivals:
    def __init__(self):
        self.copies, self.seen = {}, set()

    def __setitem__(self, key, copy):
        self.copies[key] = copy

    def wait(self, key):
        if key not in self.seen:
            self.copies[key].wait_recv()
            self.seen.add(key)
            return True
        return False


def scatter(cut, ready, done_a, done_b, ext, a_recv, a_side, b_recv, b_sum, c_recv, send):
    arrivals = Arrivals()
    slots = {}

    def take(kind, key):
        used = slots.setdefault(kind, {})
        used[key] = len(used)
        return used[key]

    def a_step(stream, way, s):
        dest = spot(way * (HOPS[stream, way] - s), stream)
        if s > 0:
            arrivals.wait(("a", stream, way, s - 1))
            held = slots["a"][stream, way, s - 1]
            a_recv[held] += ext[dest, PART_A]
            source = a_recv.at[held]
        else:
            source = ext.at[dest, PART_A]
        target = a_recv.at[take("a", (stream, way, s))]
        arrivals["a", stream, way, s] = send.copy(source, target, z_device(way))

    def a_sum(stream):
        total = ext[spot(0, stream), PART_A]
        for way in (1, -1):
            last = (stream, way, HOPS[stream, way] - 1)
            arrivals.wait(("a",) + last)
            total = total + a_recv[slots["a"][last]]
        a_side[stream] = total
        if stream > 0:
            source, target = a_side.at[stream], a_side.at[NY + stream]
            arrivals["side", stream] = send.copy(source, target, y_device(stream))

    def finish_a():
        total = a_side[0]
        for stream in (1, 3, 2):
            arrivals.wait(("side", stream))
            total = total + a_side[NY + stream]
        done_a(total)

    def b_send(offset, way, step, source):
        target = b_recv.at[take("b", (offset, way, step))]
        arrivals["b", offset, way, step] = send.copy(source, target, y_device(way))

    def b_far(offset):
        way = 1 if offset % 2 == 0 else -1
        b_send(offset, way, 0, ext.at[spot(offset, 2), PART_B])
        b_send(offset, -way, 0, ext.at[spot(offset, -way), PART_B])

    def b_near(offset):
        way = 1 if offset % 2 == 0 else -1
        arrivals.wait(("b", offset, way, 0))
        held = slots["b"][offset, way, 0]
        b_recv[held] += ext[spot(offset, way), PART_B]
        b_send(offset, way, 1, b_recv.at[held])

    def b_total(offset):
        way = 1 if offset % 2 == 0 else -1
        total = ext[spot(offset, 0), PART_B]
        for key in ((offset, way, 1), (offset, -way, 0)):
            arrivals.wait(("b",) + key)
            total = total + b_recv[slots["b"][key]]
        b_sum[offset % NZ] = total

    def c_step(away, way):
        slot = 2 * (away - 1) + (way < 0)
        part = pl.ds(half_of(way), HALF_B) if away == 4 else ALL_B
        if away < 4:
            arrivals.wait(("c", away + 1, way))
            part_held = pl.ds(half_of(way), HALF_B) if away == 3 else ALL_B
            b_sum[way * away % NZ, part_held] += c_recv[slot + 2, part_held]
        source, target = b_sum.at[way * away % NZ, part], c_recv.at[slot, part]
        arrivals["c", away, way] = send.copy(source, target, z_device(way))

    def finish_b():
        total = b_sum[0]
        for way in (1, -1):
            arrivals.wait(("c", 1, way))
            total = total + c_recv[(way < 0) + 0]
        done_b(total)

    steps = {
        "cut": cut, "a": a_step, "side": a_sum, "done_a": finish_a, "far": b_far,
        "near": b_near, "sum": b_total, "c": c_step, "done_b": finish_b,
    }
    waiting = True
    for name, *which in SCATTER_ORDER:
        if waiting and name != "cut":
            ready()
            waiting = False
        steps[name](*which)


def gather(held, keep, send):
    arrivals = Arrivals()

    def z_copy(dz, dy, part, way):
        source, target = held.at[spot(dz, dy), part], held.at[spot(dz - way, dy), part]
        return send.copy(source, target, z_device(way))

    def y_copy(dz, dy, part, way):
        source, target = held.at[spot(dz, dy), part], held.at[spot(dz, dy - way), part]
        return send.copy(source, target, y_device(way))

    def a_first():
        for step in (1, 3, 2):
            arrivals["side", step] = y_copy(0, 0, PART_A, step)

    def a_step(stream, way, s):
        if s > 0:
            arrivals.wait(("a", stream, way, s - 1))
        elif stream > 0:
            fresh = arrivals.wait(("side", stream))
        arrivals["a", stream, way, s] = z_copy(-way * s, -stream, PART_A, way)
        if s > 0 or (stream > 0 and fresh):
            keep(-way * s, -stream, PART_A)

    def a_end(stream, way):
        hops = HOPS[stream, way]
        arrivals.wait(("a", stream, way, hops - 1))
        keep(-way * hops, -stream, PART_A)

    def c_step(away, way):
        part = pl.ds(ROWS_A + half_of(way), HALF_B) if away == 4 else PART_B
        if away > 1:
            arrivals.wait(("c", away - 1, way))
        arrivals["c", away, way] = z_copy(-way * (away - 1), 0, part, way)

    def b_first(offset):
        if offset == 4:
            arrivals.wait(("c", 4, 1))
            arrivals.wait(("c", 4, -1))
        elif offset != 0:
            arrivals.wait(("c", abs(offset), 1 if offset < 0 else -1))
        for way in (1, -1):
            arrivals["b", offset, way] = y_copy(offset, 0, PART_B, way)
        if offset != 0:
            keep(offset, 0, PART_B)

    def b_second(offset):
        way = 1 if offset % 2 == 0 else -1
        arrivals.wait(("b", offset, way))
        arrivals["b", offset, 2] = y_copy(offset, -way, PART_B, way)
        keep(offset, -way, PART_B)

    def b_end(offset):
        way = 1 if offset % 2 == 0 else -1
        arrivals.wait(("b", offset, -way))
        keep(offset, way, PART_B)
        arrivals.wait(("b", offset, 2))
        keep(offset, 2, PART_B)

    steps = {
        "a_first": a_first, "a": a_step, "a_end": a_end, "c": c_step,
        "first": b_first, "second": b_second, "end": b_end,
    }
    for i, (name, *which) in enumerate(GATHER_ORDER):
        steps[name](*which)
        if i == 7:
            keep(0, 0, pl.ds(0, BOTH))


def split(value):
    high = value.astype(jnp.bfloat16)
    low = (value - high.astype(jnp.float32)).astype(jnp.bfloat16)
    return high, low


def mxu(a, b):
    return jnp.dot(a, b, preferred_element_type=jnp.float32)


def transform(fields, tables, right, left):
    halves = []
    for field in fields:
        high, low = split(jnp.concatenate(field, 1))
        halves.append(
            mxu(high, tables[right, 0])
            + (mxu(low, tables[right, 0]) + mxu(high, tables[right, 1]))
        )
    done = []
    for half in halves:
        high, low = split(jnp.concatenate([half[:, :W], half[:, W:]], 0))
        both = mxu(tables[left, 0], jnp.concatenate([high, low], 1))
        whole = both[:, :W] + (both[:, W:] + mxu(tables[left, 1], high))
        done.append((whole[:W], whole[W:]))
    return done


STEP, STEP_BACK, DFT, DFT_BACK = (0, 1), (1, 0), (2, 3), (3, 2)


def chain(trans, trans_ready, probe, counts, tables, waves, grads, grad_done):
    fields = [(probe[0, m], probe[1, m]) for m in range(MODES)]
    for j in range(DEPTH):
        trans_ready(j)
        tr, ti = trans[j, 0], trans[j, 1]
        entering = []
        for m, (real, imag) in enumerate(fields):
            waves[j, m, 0] = real
            waves[j, m, 1] = imag
            entering.append((tr * real - ti * imag, tr * imag + ti * real))
        fields = transform(entering, tables, *(STEP if j < DEPTH - 1 else DFT))
    intensity = sum(real * real + imag * imag for real, imag in fields)
    residual = intensity - count_scale * counts[0].astype(jnp.float32)
    residual = (4.0 * loss_scale) * residual
    fields = [(residual * real, residual * imag) for real, imag in fields]
    for j in reversed(range(DEPTH)):
        fields = transform(fields, tables, *(STEP_BACK if j < DEPTH - 1 else DFT_BACK))
        tr, ti = trans[j, 0], trans[j, 1]
        leaving, phase_part, absorb_part = [], 0.0, 0.0
        for m, (real, imag) in enumerate(fields):
            real, imag = tr * real + ti * imag, tr * imag - ti * real
            wr, wi = waves[j, m, 0], waves[j, m, 1]
            phase_part = phase_part + (wr * imag - wi * real)
            absorb_part = absorb_part - (wr * real + wi * imag)
            leaving.append((real, imag))
        fields = leaving
        for rows_in, kind, rows_of in BANDS:
            grads[j, rows_in] = (phase_part, absorb_part)[kind][rows_of]
        grad_done(j)


def main_kernel(
    rows_hbm, cols_hbm, slots_hbm, phase, absorb, probe_hbm, counts_hbm, tables_hbm,
    out,
    rows, cols, slots, probe, counts, tables,
    padded, ext, a_recv, a_side, b_recv, b_sum, c_recv, held,
    trans, waves, grads, got,
    load_sems, s_send, s_recv, g_send, g_recv, t_send, t_recv, d_send, d_recv, keep_sems,
):
    me = lax.axis_index("tile")
    d = lax.axis_index("depth")
    barrier = pltpu.get_barrier_semaphore()
    greeted = tile_partners()
    loads = [
        pltpu.make_async_copy(source, target, load_sems.at[i])
        for i, (source, target) in enumerate(
            [(rows_hbm, rows), (cols_hbm, cols), (slots_hbm, slots)]
            + [
                (tile.at[0, 0, :, pl.ds(c * W, W)], padded.at[m, c + 1, pl.ds(W, TS)])
                for m, tile in enumerate((phase, absorb))
                for c in range(TS // W)
            ]
            + [(probe_hbm, probe), (counts_hbm, counts), (tables_hbm, tables)]
        )
    ]
    for load in loads[:3]:
        load.start()
    for m in range(2):
        for c in range(CHUNKS):
            if 1 <= c <= TS // W:
                padded[m, c, :W] = jnp.zeros((W, W), jnp.float32)
                padded[m, c, W + TS :] = jnp.zeros((W, W), jnp.float32)
            else:
                padded[m, c] = jnp.zeros((PADDED, W), jnp.float32)
    for load in loads[3:9]:
        load.start()
    for partner in greeted:
        pl.semaphore_signal(barrier, inc=1, device_id=partner, device_id_type=MESH)

    @pl.when(d == 0)
    def _():
        for k in range(1, DEPTH):
            pl.semaphore_signal(barrier, inc=1, device_id={"depth": k}, device_id_type=MESH)

    @pl.when(d != 0)
    def _():
        pl.semaphore_signal(barrier, inc=1, device_id={"depth": 0}, device_id_type=MESH)

    for load in loads[:9]:
        load.wait()
    top, left = tile_corner(slots, me)
    lane = lax.broadcasted_iota(jnp.int32, (W, W), 1)
    z, y = tile_place()

    def cut(dz, dy):
        p = turned(z, dz, NZ) * NY + turned(y, dy, NY)
        start = jnp.clip(rows[p] - top, -W, TS) + W
        column = jnp.clip(cols[p] - left, -W, TS) + W
        chunk = lax.shift_right_logical(column, 7)
        after = jnp.minimum(chunk + 1, CHUNKS - 1)
        shift = column - chunk * W
        back = lax.bitwise_and(W - shift, W - 1)
        for m in range(2):
            first = padded[m, chunk, pl.ds(start, W), :]
            second = padded[m, after, pl.ds(start, W), :]
            moved = pltpu.roll(jnp.where(lane >= shift, first, second), back, 1)
            for rows_in, kind, rows_of in BANDS:
                if kind == m:
                    ext[spot(dz, dy), rows_in] = moved[rows_of]

    def ready():
        pl.semaphore_wait(barrier, len(greeted) + jnp.where(d == 0, DEPTH - 1, 1))
        for load in loads[9:]:
            load.start()

    send = Sender(s_send, s_recv)

    def trans_copy(j, part):
        rows_of = pl.ds(0, PIXELS) if part == 0 else pl.ds(PIXELS, REST)
        return pltpu.make_async_remote_copy(
            src_ref=trans.at[j, :, rows_of],
            dst_ref=trans.at[j, :, rows_of],
            send_sem=t_send.at[part],
            recv_sem=t_recv.at[part, j],
            device_id={"depth": 0},
            device_id_type=MESH,
        )

    def done(part):
        def put(total):
            rows_of = slice(0, PIXELS) if part == 0 else slice(PIXELS, W)
            count = total.shape[0] // 2
            damping = jnp.exp(-total[count:])
            trans[d, 0, rows_of] = damping * jnp.cos(total[:count])
            trans[d, 1, rows_of] = damping * jnp.sin(total[:count])

            @pl.when(d != 0)
            def _():
                trans_copy(d, part).start()

        return put

    scatter(
        cut, ready, done(0), done(1), ext, a_recv, a_side, b_recv, b_sum, c_recv, send
    )

    def grad_copy(j):
        return pltpu.make_async_remote_copy(
            src_ref=grads.at[j],
            dst_ref=got,
            send_sem=d_send.at[j],
            recv_sem=d_recv.at[0],
            device_id={"depth": j},
            device_id_type=MESH,
        )

    @pl.when(d == 0)
    def _():
        for load in loads[9:]:
            load.wait()

        def trans_ready(j):
            if j > 0:
                for part in range(2):
                    pltpu.make_async_remote_copy(
                        src_ref=trans.at[j, :, pl.ds(part * PIXELS, (PIXELS, REST)[part])],
                        dst_ref=trans.at[j, :, pl.ds(part * PIXELS, (PIXELS, REST)[part])],
                        send_sem=t_send.at[part],
                        recv_sem=t_recv.at[part, j],
                        device_id={"depth": 1},
                        device_id_type=MESH,
                    ).wait_recv()

        def grad_done(j):
            if j > 0:
                grad_copy(j).start()
            else:
                held[0] = grads[0]

        chain(trans, trans_ready, probe, counts, tables, waves, grads, grad_done)

    @pl.when(d != 0)
    def _():
        for load in loads[9:]:
            load.wait()
        for part in range(2):
            trans_copy(d, part).wait_send()
        pltpu.make_async_remote_copy(
            src_ref=got,
            dst_ref=got,
            send_sem=d_send.at[0],
            recv_sem=d_recv.at[0],
            device_id={"depth": 0},
            device_id_type=MESH,
        ).wait_recv()
        held[0] = got[...]

    send_back = Sender(g_send, g_recv)
    kept = []

    def keep(dz, dy, part):
        place = spot(dz, dy)
        copy = pltpu.make_async_copy(
            held.at[place, part], out.at[place, part], keep_sems.at[len(kept)]
        )
        copy.start()
        kept.append(copy)

    gather(held, keep, send_back)

    @pl.when(d == 0)
    def _():
        for j in range(1, DEPTH):
            grad_copy(j).wait_send()

    send.finish()
    send_back.finish()
    for copy in kept:
        copy.wait()


def local(phase, absorb, probe, row_offsets, col_offsets, tile_slot, counts):
    f32 = jnp.float32
    mib = 1 << 20
    dma = pltpu.SemaphoreType.DMA
    tables = jnp.asarray(make_tables())
    gathered = pl.pallas_call(
        main_kernel,
        out_shape=jax.ShapeDtypeStruct((POS, BOTH, W), f32),
        in_specs=[HBM] * 8,
        out_specs=HBM,
        scratch_shapes=[
            pltpu.SMEM((POS,), jnp.int32),
            pltpu.SMEM((POS,), jnp.int32),
            pltpu.SMEM((POS,), jnp.int32),
            pltpu.VMEM(probe.shape, f32),
            pltpu.VMEM(counts.shape, jnp.int32),
            pltpu.VMEM(tables.shape, jnp.bfloat16),
            pltpu.VMEM((2, CHUNKS, PADDED, W), f32),
            pltpu.VMEM((POS, BOTH, W), f32),
            pltpu.VMEM((28, ROWS_A, W), f32),
            pltpu.VMEM((2 * NY, ROWS_A, W), f32),
            pltpu.VMEM((24, ROWS_B, W), f32),
            pltpu.VMEM((NZ, ROWS_B, W), f32),
            pltpu.VMEM((8, ROWS_B, W), f32),
            pltpu.VMEM((POS, BOTH, W), f32),
            pltpu.VMEM((DEPTH, 2, W, W), f32),
            pltpu.VMEM((DEPTH, MODES, 2, W, W), f32),
            pltpu.VMEM((DEPTH, BOTH, W), f32),
            pltpu.VMEM((BOTH, W), f32),
            dma((12,)),
            dma((SCATTER_COPIES,)),
            dma((SCATTER_COPIES,)),
            dma((GATHER_COPIES,)),
            dma((GATHER_COPIES,)),
            dma((2,)),
            dma((2, DEPTH)),
            dma((DEPTH,)),
            dma((1,)),
            dma((2 * POS,)),
        ],
        compiler_params=pltpu.CompilerParams(
            collective_id=0, has_side_effects=True, vmem_limit_bytes=60 * mib
        ),
        name="main",
    )(row_offsets, col_offsets, tile_slot, phase, absorb, probe, counts, tables)
    return pl.pallas_call(
        deposit_kernel,
        out_shape=(jax.ShapeDtypeStruct((1, 1, TS, TS), f32),) * 2,
        in_specs=[SMEM, SMEM, SMEM, ANY],
        out_specs=(VMEM, VMEM),
        scratch_shapes=[
            pltpu.VMEM((2, TS // W + 2, PADDED, W), f32),
            pltpu.VMEM((POS, BOTH, W), f32),
            dma((POS,)),
        ],
        compiler_params=pltpu.CompilerParams(vmem_limit_bytes=60 * mib),
        name="deposit",
    )(row_offsets, col_offsets, tile_slot, gathered)


def solution(mesh):
    in_specs = (
        P("depth", "tile", None, None),
        P("depth", "tile", None, None),
        P(),
        P(),
        P(),
        P(),
        P("tile", None, None),
    )
    out_specs = (P("depth", "tile", None, None), P("depth", "tile", None, None))
    return jax.shard_map(local, mesh=mesh, in_specs=in_specs, out_specs=out_specs, check_vma=False)
```

```python
import functools
import math

import numpy as np
import jax
import jax.numpy as jnp
from jax import lax
from jax.experimental import pallas as pl
from jax.experimental.pallas import tpu as pltpu
from jax.sharding import PartitionSpec as P

W = 128
MODES = 4
TS = 384
GY = 4
POS = 32
NZ = 8
NY = 4
DEPTH = 8
BOTH = 2 * W
PIXELS = 56
ROWS_A = 2 * PIXELS
ROWS_B = BOTH - ROWS_A
HALF_B = ROWS_B // 2
REST = W - PIXELS
BANDS = (
    (slice(0, PIXELS), 0, slice(0, PIXELS)),
    (slice(PIXELS, ROWS_A), 1, slice(0, PIXELS)),
    (slice(ROWS_A, ROWS_A + REST), 0, slice(PIXELS, W)),
    (slice(ROWS_A + REST, BOTH), 1, slice(PIXELS, W)),
)
CHUNKS = TS // W + 2
PADDED = TS + 2 * W

count_scale = 0.0078125
loss_scale = 0.03125
fresnel_strength = 40.0

VMEM = pl.BlockSpec(memory_space=pltpu.VMEM)
SMEM = pl.BlockSpec(memory_space=pltpu.SMEM)
HBM = pl.BlockSpec(memory_space=pltpu.HBM)
ANY = pl.BlockSpec(memory_space=pl.ANY)
MESH = pl.DeviceIdType.MESH


def make_tables():
    index = np.arange(W)
    angle = 2.0 * np.pi * ((index[:, None] * index[None, :]) % W) / W
    dft = np.exp(-1j * angle) / math.sqrt(W)
    signed = ((index + W // 2) % W - W // 2) / W
    chirp = np.exp(-1j * fresnel_strength * signed**2)
    step = np.conj(dft) @ (chirp[:, None] * dft)
    tables = []
    for g in (step, dft):
        right = np.block([[g.real, g.imag], [-g.imag, g.real]])
        for table in (right, right.T):
            table = table.astype(np.float32)
            high = table.astype(jnp.bfloat16)
            low = (table - high.astype(np.float32)).astype(jnp.bfloat16)
            tables.append(np.stack([high, low]))
    return np.stack(tables)


def tile_corner(slots, me):
    def look(i, place):
        return jnp.where(slots[i] == me, i, place)

    place = lax.fori_loop(0, POS, look, jnp.int32(0))
    row = lax.shift_right_logical(place, 2)
    return row * TS, (place - row * GY) * TS


def overlap(rows, cols, p, top, left):
    dr = rows[p] - top
    dc = cols[p] - left
    return dr, dc, (dr > -W) & (dr < TS) & (dc > -W) & (dc < TS)


def deposit_kernel(rows, cols, slots, grads, phase_out, absorb_out, acc, found, sems):
    me = lax.axis_index("tile")
    top, left = tile_corner(slots, me)
    z, y = tile_place()
    lane = lax.broadcasted_iota(jnp.int32, (W, W), 1)

    def look(p, count):
        found[count] = p
        dr, dc, touches = overlap(rows, cols, p, top, left)
        return count + jnp.where(touches, 1, 0)

    count = lax.fori_loop(0, POS, look, jnp.int32(0))
    copies = []
    for m, target in enumerate((phase_out, absorb_out)):
        acc[m, 1 : CHUNKS - 1, W : W + TS] = jnp.zeros((CHUNKS - 2, TS, W), jnp.float32)

        def one(i, carry, m=m):
            p = found[i]
            row = lax.shift_right_logical(p, 2)
            place = turned(row, -z, NZ) * NY + turned(p - row * NY, -y, NY)
            start = rows[p] - top + W
            column = cols[p] - left + W
            chunk = lax.shift_right_logical(column, 7)
            shift = column - chunk * W
            pieces = [grads[place, rows_in] for rows_in, kind, _ in BANDS if kind == m]
            moved = pltpu.roll(jnp.concatenate(pieces, 0), shift, 1)
            acc[m, chunk, pl.ds(start, W), :] += jnp.where(lane >= shift, moved, 0.0)
            acc[m, chunk + 1, pl.ds(start, W), :] += jnp.where(lane < shift, moved, 0.0)
            return carry

        lax.fori_loop(0, count, one, 0)
        for c in range(TS // W):
            copy = pltpu.make_async_copy(
                acc.at[m, c + 1, pl.ds(W, TS)],
                target.at[0, 0, :, pl.ds(c * W, W)],
                sems.at[len(copies)],
            )
            copy.start()
            copies.append(copy)
    for copy in copies:
        copy.wait()


def tile_place():
    me = lax.axis_index("tile")
    z = me // NY
    return z, me - z * NY


def turned(value, step, count):
    return lax.rem(value + step + count, count)


def z_device(way):
    z, y = tile_place()
    return {"tile": turned(z, way, NZ) * NY + y}


def y_device(step):
    z, y = tile_place()
    return {"tile": z * NY + turned(y, step, NY)}


def tile_partners():
    return [z_device(k) for k in (1, -1, 2, -2)] + [y_device(k) for k in range(1, NY)]


class Sender:
    def __init__(self, send_sems, recv_sems):
        self.send_sems, self.recv_sems = send_sems, recv_sems
        self.started = []

    def copy(self, source, target, device):
        n = len(self.started)
        copy = pltpu.make_async_remote_copy(
            src_ref=source,
            dst_ref=target,
            send_sem=self.send_sems.at[n],
            recv_sem=self.recv_sems.at[n],
            device_id=device,
            device_id_type=MESH,
        )
        copy.start()
        self.started.append(copy)
        return copy

    def finish(self):
        for copy in self.started:
            copy.wait_send()


HOPS = {
    (0, 1): 4, (1, 1): 4, (2, -1): 4, (3, -1): 4, (2, 1): 3, (3, 1): 3, (0, -1): 3, (1, -1): 3,
}
SCATTER_ORDER = (
    ("cut", 4, 1), ("cut", 4, 3), ("cut", 4, 2), ("far", 4), ("cut", 3, 2), ("a", 1, 1, 0),
    ("a", 3, -1, 0), ("cut", -1, 2), ("a", 2, 1, 0), ("cut", -3, 0), ("cut", -3, 2),
    ("cut", 3, 1), ("a", 2, -1, 0), ("cut", -2, 3), ("cut", -3, 1), ("far", 3), ("cut", 3, 3),
    ("cut", -2, 1), ("far", -3), ("cut", 4, 0), ("cut", -1, 0), ("a", 3, 1, 0), ("cut", -1, 3),
    ("a", 1, -1, 0), ("cut", 3, 0), ("cut", 1, 1), ("a", 0, 1, 0), ("cut", 0, 2), ("cut", -2, 0),
    ("a", 0, -1, 0), ("cut", -2, 2), ("near", 4), ("cut", -3, 3), ("cut", 2, 0), ("a", 1, 1, 1),
    ("cut", 0, 1), ("cut", 2, 1), ("cut", 1, 2), ("far", -2), ("a", 2, -1, 1), ("cut", 2, 3),
    ("cut", 0, 3), ("a", 1, -1, 1), ("near", -3), ("a", 3, 1, 1), ("a", 3, -1, 1), ("cut", 2, 2),
    ("a", 0, -1, 1), ("a", 0, 1, 1), ("a", 1, 1, 2), ("far", 2), ("sum", 4), ("near", 3),
    ("c", 4, 1), ("a", 2, 1, 1), ("near", -2), ("cut", -1, 1), ("a", 2, -1, 2), ("c", 4, -1),
    ("far", -1), ("sum", -3), ("near", 2), ("a", 3, -1, 2), ("cut", 1, 3), ("a", 3, 1, 2),
    ("cut", 0, 0), ("a", 1, -1, 2), ("far", 0), ("a", 1, 1, 3), ("c", 3, -1), ("sum", 3),
    ("c", 3, 1), ("far", 1), ("a", 3, -1, 3), ("a", 2, 1, 2), ("near", -1), ("a", 2, -1, 3),
    ("side", 1), ("sum", -2), ("a", 0, 1, 2), ("c", 2, -1), ("sum", 2), ("near", 1), ("c", 2, 1),
    ("near", 0), ("side", 3), ("a", 0, -1, 2), ("sum", -1), ("cut", 1, 0), ("a", 0, 1, 3),
    ("side", 2), ("sum", 1), ("c", 1, -1), ("c", 1, 1), ("sum", 0), ("side", 0), ("done_a",),
    ("done_b",),
)
GATHER_ORDER = (
    ("c", 1, 1), ("c", 1, -1), ("a_first",), ("first", 0), ("a", 0, -1, 0), ("a", 0, 1, 0),
    ("c", 2, 1), ("first", -1), ("c", 2, -1), ("a", 2, 1, 0), ("a", 0, -1, 1), ("a", 3, -1, 0),
    ("a", 0, 1, 1), ("first", -2), ("second", 0), ("c", 3, 1), ("a", 2, -1, 0), ("first", 2),
    ("first", 1), ("a", 1, 1, 0), ("c", 3, -1), ("second", -1), ("a", 3, -1, 1), ("a", 2, 1, 1),
    ("a", 3, 1, 0), ("a", 2, -1, 1), ("a", 1, -1, 0), ("a", 0, 1, 2), ("first", -3),
    ("a", 1, 1, 1), ("a", 3, -1, 2), ("c", 4, 1), ("first", 3), ("c", 4, -1), ("a", 3, 1, 1),
    ("a", 2, -1, 2), ("second", 1), ("second", 2), ("a", 2, 1, 2), ("end", -1), ("a", 1, -1, 1),
    ("a", 1, 1, 2), ("first", 4), ("a", 0, -1, 2), ("second", 3), ("a", 3, 1, 2), ("a", 0, 1, 3),
    ("second", -2), ("a", 3, -1, 3), ("a", 1, -1, 2), ("end", 2), ("end", 0), ("end", 1),
    ("second", -3), ("a", 2, -1, 3), ("a", 1, 1, 3), ("second", 4), ("a_end", 0, 1), ("end", 3),
    ("end", -2), ("a_end", 0, -1), ("a_end", 3, 1), ("a_end", 3, -1), ("end", -3),
    ("a_end", 1, -1), ("a_end", 2, 1), ("a_end", 1, 1), ("end", 4), ("a_end", 2, -1),
)
SCATTER_COPIES = 28 + 3 + 24 + 8
GATHER_COPIES = 28 + 3 + 24 + 8
PART_A = pl.ds(0, ROWS_A)
PART_B = pl.ds(ROWS_A, ROWS_B)
ALL_B = pl.ds(0, ROWS_B)


def half_of(way):
    return 0 if way == 1 else HALF_B


def spot(dz, dy):
    return (dz % NZ) * NY + dy % NY


class Arrivals:
    def __init__(self):
        self.copies, self.seen = {}, set()

    def __setitem__(self, key, copy):
        self.copies[key] = copy

    def wait(self, key):
        if key not in self.seen:
            self.copies[key].wait_recv()
            self.seen.add(key)
            return True
        return False


def scatter(cut, ready, done_a, done_b, ext, a_recv, a_side, b_recv, b_sum, c_recv, send):
    arrivals = Arrivals()
    slots = {}

    def take(kind, key):
        used = slots.setdefault(kind, {})
        used[key] = len(used)
        return used[key]

    def a_step(stream, way, s):
        dest = spot(way * (HOPS[stream, way] - s), stream)
        if s > 0:
            arrivals.wait(("a", stream, way, s - 1))
            held = slots["a"][stream, way, s - 1]
            a_recv[held] += ext[dest, PART_A]
            source = a_recv.at[held]
        else:
            source = ext.at[dest, PART_A]
        target = a_recv.at[take("a", (stream, way, s))]
        arrivals["a", stream, way, s] = send.copy(source, target, z_device(way))

    def a_sum(stream):
        total = ext[spot(0, stream), PART_A]
        for way in (1, -1):
            last = (stream, way, HOPS[stream, way] - 1)
            arrivals.wait(("a",) + last)
            total = total + a_recv[slots["a"][last]]
        a_side[stream] = total
        if stream > 0:
            source, target = a_side.at[stream], a_side.at[NY + stream]
            arrivals["side", stream] = send.copy(source, target, y_device(stream))

    def finish_a():
        total = a_side[0]
        for stream in (1, 3, 2):
            arrivals.wait(("side", stream))
            total = total + a_side[NY + stream]
        done_a(total)

    def b_send(offset, way, step, source):
        target = b_recv.at[take("b", (offset, way, step))]
        arrivals["b", offset, way, step] = send.copy(source, target, y_device(way))

    def b_far(offset):
        way = 1 if offset % 2 == 0 else -1
        b_send(offset, way, 0, ext.at[spot(offset, 2), PART_B])
        b_send(offset, -way, 0, ext.at[spot(offset, -way), PART_B])

    def b_near(offset):
        way = 1 if offset % 2 == 0 else -1
        arrivals.wait(("b", offset, way, 0))
        held = slots["b"][offset, way, 0]
        b_recv[held] += ext[spot(offset, way), PART_B]
        b_send(offset, way, 1, b_recv.at[held])

    def b_total(offset):
        way = 1 if offset % 2 == 0 else -1
        total = ext[spot(offset, 0), PART_B]
        for key in ((offset, way, 1), (offset, -way, 0)):
            arrivals.wait(("b",) + key)
            total = total + b_recv[slots["b"][key]]
        b_sum[offset % NZ] = total

    def c_step(away, way):
        slot = 2 * (away - 1) + (way < 0)
        part = pl.ds(half_of(way), HALF_B) if away == 4 else ALL_B
        if away < 4:
            arrivals.wait(("c", away + 1, way))
            part_held = pl.ds(half_of(way), HALF_B) if away == 3 else ALL_B
            b_sum[way * away % NZ, part_held] += c_recv[slot + 2, part_held]
        source, target = b_sum.at[way * away % NZ, part], c_recv.at[slot, part]
        arrivals["c", away, way] = send.copy(source, target, z_device(way))

    def finish_b():
        total = b_sum[0]
        for way in (1, -1):
            arrivals.wait(("c", 1, way))
            total = total + c_recv[(way < 0) + 0]
        done_b(total)

    steps = {
        "cut": cut, "a": a_step, "side": a_sum, "done_a": finish_a, "far": b_far,
        "near": b_near, "sum": b_total, "c": c_step, "done_b": finish_b,
    }
    waiting = True
    for name, *which in SCATTER_ORDER:
        if waiting and name != "cut":
            ready()
            waiting = False
        steps[name](*which)


def gather(held, send):
    arrivals = Arrivals()

    def z_copy(dz, dy, part, way):
        source, target = held.at[spot(dz, dy), part], held.at[spot(dz - way, dy), part]
        return send.copy(source, target, z_device(way))

    def y_copy(dz, dy, part, way):
        source, target = held.at[spot(dz, dy), part], held.at[spot(dz, dy - way), part]
        return send.copy(source, target, y_device(way))

    def a_first():
        for step in (1, 3, 2):
            arrivals["side", step] = y_copy(0, 0, PART_A, step)

    def a_step(stream, way, s):
        if s > 0:
            arrivals.wait(("a", stream, way, s - 1))
        elif stream > 0:
            arrivals.wait(("side", stream))
        arrivals["a", stream, way, s] = z_copy(-way * s, -stream, PART_A, way)

    def a_end(stream, way):
        hops = HOPS[stream, way]
        arrivals.wait(("a", stream, way, hops - 1))

    def c_step(away, way):
        part = pl.ds(ROWS_A + half_of(way), HALF_B) if away == 4 else PART_B
        if away > 1:
            arrivals.wait(("c", away - 1, way))
        arrivals["c", away, way] = z_copy(-way * (away - 1), 0, part, way)

    def b_first(offset):
        if offset == 4:
            arrivals.wait(("c", 4, 1))
            arrivals.wait(("c", 4, -1))
        elif offset != 0:
            arrivals.wait(("c", abs(offset), 1 if offset < 0 else -1))
        for way in (1, -1):
            arrivals["b", offset, way] = y_copy(offset, 0, PART_B, way)

    def b_second(offset):
        way = 1 if offset % 2 == 0 else -1
        arrivals.wait(("b", offset, way))
        arrivals["b", offset, 2] = y_copy(offset, -way, PART_B, way)

    def b_end(offset):
        way = 1 if offset % 2 == 0 else -1
        arrivals.wait(("b", offset, -way))
        arrivals.wait(("b", offset, 2))

    steps = {
        "a_first": a_first, "a": a_step, "a_end": a_end, "c": c_step,
        "first": b_first, "second": b_second, "end": b_end,
    }
    for name, *which in GATHER_ORDER:
        steps[name](*which)


def split(value):
    high = value.astype(jnp.bfloat16)
    low = (value - high.astype(jnp.float32)).astype(jnp.bfloat16)
    return high, low


def mxu(a, b):
    return jnp.dot(a, b, preferred_element_type=jnp.float32)


def transform(fields, tables, right, left):
    halves = []
    for field in fields:
        high, low = split(jnp.concatenate(field, 1))
        halves.append(
            mxu(high, tables[right, 0])
            + (mxu(low, tables[right, 0]) + mxu(high, tables[right, 1]))
        )
    done = []
    for half in halves:
        high, low = split(jnp.concatenate([half[:, :W], half[:, W:]], 0))
        both = mxu(tables[left, 0], jnp.concatenate([high, low], 1))
        whole = both[:, :W] + (both[:, W:] + mxu(tables[left, 1], high))
        done.append((whole[:W], whole[W:]))
    return done


STEP, STEP_BACK, DFT, DFT_BACK = (0, 1), (1, 0), (2, 3), (3, 2)


def chain(trans, trans_ready, probe, counts, tables, waves, grads, own, grad_done):
    fields = [(probe[0, m], probe[1, m]) for m in range(MODES)]
    for j in range(DEPTH):
        trans_ready(j)
        tr, ti = trans[j, 0], trans[j, 1]
        entering = []
        for m, (real, imag) in enumerate(fields):
            waves[j, m, 0] = real
            waves[j, m, 1] = imag
            entering.append((tr * real - ti * imag, tr * imag + ti * real))
        fields = transform(entering, tables, *(STEP if j < DEPTH - 1 else DFT))
    intensity = sum(real * real + imag * imag for real, imag in fields)
    residual = intensity - count_scale * counts[0].astype(jnp.float32)
    residual = (4.0 * loss_scale) * residual
    fields = [(residual * real, residual * imag) for real, imag in fields]
    for j in reversed(range(DEPTH)):
        fields = transform(fields, tables, *(STEP_BACK if j < DEPTH - 1 else DFT_BACK))
        tr, ti = trans[j, 0], trans[j, 1]
        leaving, phase_part, absorb_part = [], 0.0, 0.0
        for m, (real, imag) in enumerate(fields):
            real, imag = tr * real + ti * imag, tr * imag - ti * real
            wr, wi = waves[j, m, 0], waves[j, m, 1]
            phase_part = phase_part + (wr * imag - wi * real)
            absorb_part = absorb_part - (wr * real + wi * imag)
            leaving.append((real, imag))
        fields = leaving
        target = grads.at[j] if j > 0 else own
        for rows_in, kind, rows_of in BANDS:
            target[rows_in] = (phase_part, absorb_part)[kind][rows_of]
        grad_done(j)


def main_kernel(
    rows_hbm, cols_hbm, slots_hbm, phase, absorb, probe_hbm, counts_hbm, tables_hbm,
    held,
    rows, cols, slots, probe, counts, tables,
    padded, ext, a_recv, a_side, b_recv, b_sum, c_recv,
    trans, waves, grads,
    load_sems, s_send, s_recv, g_send, g_recv, t_send, t_recv, d_send, d_recv,
):
    me = lax.axis_index("tile")
    d = lax.axis_index("depth")
    barrier = pltpu.get_barrier_semaphore()
    greeted = tile_partners()
    loads = [
        pltpu.make_async_copy(source, target, load_sems.at[i])
        for i, (source, target) in enumerate(
            [(rows_hbm, rows), (cols_hbm, cols), (slots_hbm, slots)]
            + [
                (tile.at[0, 0, :, pl.ds(c * W, W)], padded.at[m, c + 1, pl.ds(W, TS)])
                for m, tile in enumerate((phase, absorb))
                for c in range(TS // W)
            ]
            + [(probe_hbm, probe), (counts_hbm, counts), (tables_hbm, tables)]
        )
    ]
    for load in loads[:3]:
        load.start()
    for m in range(2):
        for c in range(CHUNKS):
            if 1 <= c <= TS // W:
                padded[m, c, :W] = jnp.zeros((W, W), jnp.float32)
                padded[m, c, W + TS :] = jnp.zeros((W, W), jnp.float32)
            else:
                padded[m, c] = jnp.zeros((PADDED, W), jnp.float32)
    for load in loads[3:9]:
        load.start()
    for partner in greeted:
        pl.semaphore_signal(barrier, inc=1, device_id=partner, device_id_type=MESH)

    @pl.when(d == 0)
    def _():
        for k in range(1, DEPTH):
            pl.semaphore_signal(barrier, inc=1, device_id={"depth": k}, device_id_type=MESH)

    @pl.when(d != 0)
    def _():
        pl.semaphore_signal(barrier, inc=1, device_id={"depth": 0}, device_id_type=MESH)

    for load in loads[:9]:
        load.wait()
    top, left = tile_corner(slots, me)
    lane = lax.broadcasted_iota(jnp.int32, (W, W), 1)
    z, y = tile_place()

    def cut(dz, dy):
        p = turned(z, dz, NZ) * NY + turned(y, dy, NY)
        start = jnp.clip(rows[p] - top, -W, TS) + W
        column = jnp.clip(cols[p] - left, -W, TS) + W
        chunk = lax.shift_right_logical(column, 7)
        after = jnp.minimum(chunk + 1, CHUNKS - 1)
        shift = column - chunk * W
        back = lax.bitwise_and(W - shift, W - 1)
        for m in range(2):
            first = padded[m, chunk, pl.ds(start, W), :]
            second = padded[m, after, pl.ds(start, W), :]
            moved = pltpu.roll(jnp.where(lane >= shift, first, second), back, 1)
            for rows_in, kind, rows_of in BANDS:
                if kind == m:
                    ext[spot(dz, dy), rows_in] = moved[rows_of]

    def ready():
        pl.semaphore_wait(barrier, len(greeted) + jnp.where(d == 0, DEPTH - 1, 1))
        for load in loads[9:]:
            load.start()

    send = Sender(s_send, s_recv)

    def trans_copy(j, part):
        rows_of = pl.ds(0, PIXELS) if part == 0 else pl.ds(PIXELS, REST)
        return pltpu.make_async_remote_copy(
            src_ref=trans.at[j, :, rows_of],
            dst_ref=trans.at[j, :, rows_of],
            send_sem=t_send.at[part],
            recv_sem=t_recv.at[part, j],
            device_id={"depth": 0},
            device_id_type=MESH,
        )

    def done(part):
        def put(total):
            rows_of = slice(0, PIXELS) if part == 0 else slice(PIXELS, W)
            count = total.shape[0] // 2
            damping = jnp.exp(-total[count:])
            trans[d, 0, rows_of] = damping * jnp.cos(total[:count])
            trans[d, 1, rows_of] = damping * jnp.sin(total[:count])

            @pl.when(d != 0)
            def _():
                trans_copy(d, part).start()

        return put

    scatter(
        cut, ready, done(0), done(1), ext, a_recv, a_side, b_recv, b_sum, c_recv, send
    )

    def grad_copy(j):
        return pltpu.make_async_remote_copy(
            src_ref=grads.at[j],
            dst_ref=held.at[0],
            send_sem=d_send.at[j],
            recv_sem=d_recv.at[0],
            device_id={"depth": j},
            device_id_type=MESH,
        )

    @pl.when(d == 0)
    def _():
        for load in loads[9:]:
            load.wait()

        def trans_ready(j):
            if j > 0:
                for part in range(2):
                    pltpu.make_async_remote_copy(
                        src_ref=trans.at[j, :, pl.ds(part * PIXELS, (PIXELS, REST)[part])],
                        dst_ref=trans.at[j, :, pl.ds(part * PIXELS, (PIXELS, REST)[part])],
                        send_sem=t_send.at[part],
                        recv_sem=t_recv.at[part, j],
                        device_id={"depth": 1},
                        device_id_type=MESH,
                    ).wait_recv()

        def grad_done(j):
            if j > 0:
                grad_copy(j).start()

        chain(trans, trans_ready, probe, counts, tables, waves, grads, held.at[0], grad_done)

    @pl.when(d != 0)
    def _():
        for load in loads[9:]:
            load.wait()
        for part in range(2):
            trans_copy(d, part).wait_send()
        pltpu.make_async_remote_copy(
            src_ref=held.at[0],
            dst_ref=held.at[0],
            send_sem=d_send.at[0],
            recv_sem=d_recv.at[0],
            device_id={"depth": 0},
            device_id_type=MESH,
        ).wait_recv()

    send_back = Sender(g_send, g_recv)
    gather(held, send_back)

    @pl.when(d == 0)
    def _():
        for j in range(1, DEPTH):
            grad_copy(j).wait_send()

    send.finish()
    send_back.finish()


def local(phase, absorb, probe, row_offsets, col_offsets, tile_slot, counts):
    f32 = jnp.float32
    mib = 1 << 20
    dma = pltpu.SemaphoreType.DMA
    tables = jnp.asarray(make_tables())
    gathered = pl.pallas_call(
        main_kernel,
        out_shape=jax.ShapeDtypeStruct((POS, BOTH, W), f32),
        in_specs=[HBM] * 8,
        out_specs=VMEM,
        scratch_shapes=[
            pltpu.SMEM((POS,), jnp.int32),
            pltpu.SMEM((POS,), jnp.int32),
            pltpu.SMEM((POS,), jnp.int32),
            pltpu.VMEM(probe.shape, f32),
            pltpu.VMEM(counts.shape, jnp.int32),
            pltpu.VMEM(tables.shape, jnp.bfloat16),
            pltpu.VMEM((2, CHUNKS, PADDED, W), f32),
            pltpu.VMEM((POS, BOTH, W), f32),
            pltpu.VMEM((28, ROWS_A, W), f32),
            pltpu.VMEM((2 * NY, ROWS_A, W), f32),
            pltpu.VMEM((24, ROWS_B, W), f32),
            pltpu.VMEM((NZ, ROWS_B, W), f32),
            pltpu.VMEM((8, ROWS_B, W), f32),
            pltpu.VMEM((DEPTH, 2, W, W), f32),
            pltpu.VMEM((DEPTH, MODES, 2, W, W), f32),
            pltpu.VMEM((DEPTH, BOTH, W), f32),
            dma((12,)),
            dma((SCATTER_COPIES,)),
            dma((SCATTER_COPIES,)),
            dma((GATHER_COPIES,)),
            dma((GATHER_COPIES,)),
            dma((2,)),
            dma((2, DEPTH)),
            dma((DEPTH,)),
            dma((1,)),
        ],
        compiler_params=pltpu.CompilerParams(
            collective_id=0, has_side_effects=True, vmem_limit_bytes=40 * mib
        ),
        name="main",
    )(*(
        pltpu.with_memory_space_constraint(v, pltpu.HBM)
        for v in (row_offsets, col_offsets, tile_slot, phase, absorb, probe, counts, tables)
    ))
    return pl.pallas_call(
        deposit_kernel,
        out_shape=(jax.ShapeDtypeStruct((1, 1, TS, TS), f32),) * 2,
        in_specs=[SMEM, SMEM, SMEM, VMEM],
        out_specs=(HBM, HBM),
        scratch_shapes=[
            pltpu.VMEM((2, CHUNKS, PADDED, W), f32),
            pltpu.SMEM((POS,), jnp.int32),
            dma((2 * (CHUNKS - 2),)),
        ],
        compiler_params=pltpu.CompilerParams(vmem_limit_bytes=24 * mib),
        name="deposit",
    )(row_offsets, col_offsets, tile_slot, gathered)


def solution(mesh):
    in_specs = (
        P("depth", "tile", None, None),
        P("depth", "tile", None, None),
        P(),
        P(),
        P(),
        P(),
        P("tile", None, None),
    )
    out_specs = (P("depth", "tile", None, None), P("depth", "tile", None, None))
    return jax.shard_map(local, mesh=mesh, in_specs=in_specs, out_specs=out_specs, check_vma=False)
```

```python
import functools
import math

import numpy as np
import jax
import jax.numpy as jnp
from jax import lax
from jax.experimental import pallas as pl
from jax.experimental.pallas import tpu as pltpu
from jax.sharding import PartitionSpec as P

W = 128
MODES = 4
TS = 384
GY = 4
POS = 32
NZ = 8
NY = 4
DEPTH = 8
BOTH = 2 * W
PIXELS = 56
ROWS_A = 2 * PIXELS
ROWS_B = BOTH - ROWS_A
HALF_B = ROWS_B // 2
REST = W - PIXELS
BANDS = (
    (slice(0, PIXELS), 0, slice(0, PIXELS)),
    (slice(PIXELS, ROWS_A), 1, slice(0, PIXELS)),
    (slice(ROWS_A, ROWS_A + REST), 0, slice(PIXELS, W)),
    (slice(ROWS_A + REST, BOTH), 1, slice(PIXELS, W)),
)
CHUNKS = TS // W + 2
PADDED = TS + 2 * W

count_scale = 0.0078125
loss_scale = 0.03125
fresnel_strength = 40.0

VMEM = pl.BlockSpec(memory_space=pltpu.VMEM)
SMEM = pl.BlockSpec(memory_space=pltpu.SMEM)
HBM = pl.BlockSpec(memory_space=pltpu.HBM)
ANY = pl.BlockSpec(memory_space=pl.ANY)
MESH = pl.DeviceIdType.MESH


def make_tables():
    index = np.arange(W)
    angle = 2.0 * np.pi * ((index[:, None] * index[None, :]) % W) / W
    dft = np.exp(-1j * angle) / math.sqrt(W)
    signed = ((index + W // 2) % W - W // 2) / W
    chirp = np.exp(-1j * fresnel_strength * signed**2)
    step = np.conj(dft) @ (chirp[:, None] * dft)
    tables = []
    for g in (step, dft):
        right = np.block([[g.real, g.imag], [-g.imag, g.real]])
        for table in (right, right.T):
            table = table.astype(np.float32)
            high = table.astype(jnp.bfloat16)
            low = (table - high.astype(np.float32)).astype(jnp.bfloat16)
            tables.append(np.stack([high, low]))
    return np.stack(tables)


def tile_corner(slots, me):
    def look(i, place):
        return jnp.where(slots[i] == me, i, place)

    place = lax.fori_loop(0, POS, look, jnp.int32(0))
    row = lax.shift_right_logical(place, 2)
    return row * TS, (place - row * GY) * TS


def overlap(rows, cols, p, top, left):
    dr = rows[p] - top
    dc = cols[p] - left
    return dr, dc, (dr > -W) & (dr < TS) & (dc > -W) & (dc < TS)


def deposit_kernel(rows, cols, slots, grads, phase_out, absorb_out, acc, found, sems):
    me = lax.axis_index("tile")
    top, left = tile_corner(slots, me)
    z, y = tile_place()
    lane = lax.broadcasted_iota(jnp.int32, (W, W), 1)

    def look(p, count):
        found[count] = p
        dr, dc, touches = overlap(rows, cols, p, top, left)
        return count + jnp.where(touches, 1, 0)

    count = lax.fori_loop(0, POS, look, jnp.int32(0))
    copies = []
    for m, target in enumerate((phase_out, absorb_out)):
        acc[m, 1 : CHUNKS - 1, W : W + TS] = jnp.zeros((CHUNKS - 2, TS, W), jnp.float32)

        def one(i, carry, m=m):
            p = found[i]
            row = lax.shift_right_logical(p, 2)
            place = turned(row, -z, NZ) * NY + turned(p - row * NY, -y, NY)
            start = rows[p] - top + W
            column = cols[p] - left + W
            chunk = lax.shift_right_logical(column, 7)
            shift = column - chunk * W
            pieces = [grads[place, rows_in] for rows_in, kind, _ in BANDS if kind == m]
            moved = pltpu.roll(jnp.concatenate(pieces, 0), shift, 1)
            acc[m, chunk, pl.ds(start, W), :] += jnp.where(lane >= shift, moved, 0.0)
            acc[m, chunk + 1, pl.ds(start, W), :] += jnp.where(lane < shift, moved, 0.0)
            return carry

        lax.fori_loop(0, count, one, 0)
        for c in range(TS // W):
            copy = pltpu.make_async_copy(
                acc.at[m, c + 1, pl.ds(W, TS)],
                target.at[0, 0, :, pl.ds(c * W, W)],
                sems.at[len(copies)],
            )
            copy.start()
            copies.append(copy)
    for copy in copies:
        copy.wait()


def tile_place():
    me = lax.axis_index("tile")
    z = me // NY
    return z, me - z * NY


def turned(value, step, count):
    return lax.rem(value + step + count, count)


def z_device(way):
    z, y = tile_place()
    return {"tile": turned(z, way, NZ) * NY + y}


def y_device(step):
    z, y = tile_place()
    return {"tile": z * NY + turned(y, step, NY)}


def tile_partners():
    return [z_device(k) for k in (1, -1, 2, -2)] + [y_device(k) for k in range(1, NY)]


class Sender:
    def __init__(self, send_sems, recv_sems):
        self.send_sems, self.recv_sems = send_sems, recv_sems
        self.started = []

    def copy(self, source, target, device):
        n = len(self.started)
        copy = pltpu.make_async_remote_copy(
            src_ref=source,
            dst_ref=target,
            send_sem=self.send_sems.at[n],
            recv_sem=self.recv_sems.at[n],
            device_id=device,
            device_id_type=MESH,
        )
        copy.start()
        self.started.append(copy)
        return copy

    def finish(self):
        for copy in self.started:
            copy.wait_send()


HOPS = {
    (0, 1): 4, (1, 1): 4, (2, -1): 4, (3, -1): 4, (2, 1): 3, (3, 1): 3, (0, -1): 3, (1, -1): 3,
}
SCATTER_ORDER = (
    ("cut", 4, 2), ("cut", 4, 1), ("a", 1, 1, 0), ("cut", 4, 3), ("far", 4), ("cut", 2, 2),
    ("cut", 3, 3), ("a", 3, -1, 0), ("cut", -3, 1), ("cut", -3, 2), ("cut", -1, 2),
    ("a", 3, 1, 0), ("a", 2, -1, 0), ("cut", -3, 0), ("cut", 3, 2), ("cut", 3, 1), ("cut", -1, 1),
    ("far", 3), ("cut", 1, 2), ("cut", 4, 0), ("cut", 1, 3), ("cut", 0, 1), ("cut", 0, 0),
    ("a", 1, -1, 0), ("cut", -2, 1), ("far", -3), ("a", 1, 1, 1), ("cut", -3, 3), ("cut", 2, 3),
    ("a", 0, -1, 0), ("near", 4), ("a", 0, 1, 0), ("cut", 2, 0), ("cut", -2, 2), ("cut", -2, 3),
    ("cut", -2, 0), ("cut", 3, 0), ("a", 3, 1, 1), ("cut", 1, 1), ("a", 2, 1, 0), ("cut", 2, 1),
    ("a", 2, -1, 1), ("far", -2), ("near", 3), ("a", 1, -1, 1), ("cut", -1, 0), ("a", 3, -1, 1),
    ("near", -3), ("far", 2), ("a", 1, 1, 2), ("cut", 0, 2), ("a", 0, 1, 1), ("a", 0, -1, 1),
    ("sum", 4), ("far", 1), ("c", 4, -1), ("c", 4, 1), ("a", 2, -1, 2), ("near", -2),
    ("a", 2, 1, 1), ("a", 1, -1, 2), ("near", 2), ("a", 3, 1, 2), ("sum", 3), ("cut", -1, 3),
    ("a", 3, -1, 2), ("far", -1), ("cut", 0, 3), ("a", 1, 1, 3), ("c", 3, 1), ("far", 0),
    ("sum", -3), ("c", 3, -1), ("cut", 1, 0), ("sum", -2), ("near", 1), ("a", 2, -1, 3),
    ("a", 2, 1, 2), ("a", 3, -1, 3), ("a", 0, 1, 2), ("near", -1), ("sum", 2), ("c", 2, -1),
    ("c", 2, 1), ("side", 1), ("sum", 1), ("near", 0), ("side", 2), ("a", 0, -1, 2), ("side", 3),
    ("a", 0, 1, 3), ("sum", -1), ("c", 1, -1), ("c", 1, 1), ("side", 0), ("sum", 0), ("done_a",),
    ("done_b",),
)
GATHER_ORDER = (
    ("c", 1, -1), ("c", 1, 1), ("a_first",), ("a", 0, 1, 0), ("first", 0), ("a", 0, -1, 0),
    ("c", 2, -1), ("c", 2, 1), ("first", 1), ("a", 3, -1, 0), ("a", 1, -1, 0), ("first", -1),
    ("a", 2, -1, 0), ("second", 0), ("a", 1, 1, 0), ("a", 2, 1, 0), ("c", 3, 1), ("first", -2),
    ("second", 1), ("first", 2), ("a", 0, 1, 1), ("c", 3, -1), ("a", 0, -1, 1), ("a", 3, -1, 1),
    ("a", 1, 1, 1), ("a", 3, 1, 0), ("first", -3), ("c", 4, 1), ("a", 2, -1, 1), ("a", 0, 1, 2),
    ("second", -1), ("second", 2), ("c", 4, -1), ("a", 2, 1, 1), ("first", 3), ("end", 1),
    ("a", 1, -1, 1), ("a", 3, 1, 1), ("a", 2, -1, 2), ("a", 3, -1, 2), ("a", 1, 1, 2),
    ("first", 4), ("end", 0), ("a", 1, -1, 2), ("a", 0, 1, 3), ("end", -1), ("a", 2, 1, 2),
    ("second", -2), ("second", 3), ("a", 0, -1, 2), ("a", 1, 1, 3), ("a", 3, -1, 3),
    ("second", 4), ("second", -3), ("end", 2), ("a_end", 1, -1), ("a", 3, 1, 2), ("a", 2, -1, 3),
    ("end", -2), ("a_end", 0, -1), ("end", 3), ("a_end", 1, 1), ("end", -3), ("a_end", 0, 1),
    ("a_end", 3, -1), ("end", 4), ("a_end", 2, -1), ("a_end", 2, 1), ("a_end", 3, 1),
)
SCATTER_COPIES = 28 + 3 + 24 + 8
GATHER_COPIES = 28 + 3 + 24 + 8
PART_A = pl.ds(0, ROWS_A)
PART_B = pl.ds(ROWS_A, ROWS_B)
ALL_B = pl.ds(0, ROWS_B)


def half_of(way):
    return 0 if way == 1 else HALF_B


def spot(dz, dy):
    return (dz % NZ) * NY + dy % NY


class Arrivals:
    def __init__(self):
        self.copies, self.seen = {}, set()

    def __setitem__(self, key, copy):
        self.copies[key] = copy

    def wait(self, key):
        if key not in self.seen:
            self.copies[key].wait_recv()
            self.seen.add(key)
            return True
        return False


def scatter(cut, ready, done_a, done_b, ext, a_recv, a_side, b_recv, b_sum, c_recv, send):
    arrivals = Arrivals()
    slots = {}

    def take(kind, key):
        used = slots.setdefault(kind, {})
        used[key] = len(used)
        return used[key]

    def a_step(stream, way, s):
        dest = spot(way * (HOPS[stream, way] - s), stream)
        if s > 0:
            arrivals.wait(("a", stream, way, s - 1))
            held = slots["a"][stream, way, s - 1]
            a_recv[held] += ext[dest, PART_A]
            source = a_recv.at[held]
        else:
            source = ext.at[dest, PART_A]
        target = a_recv.at[take("a", (stream, way, s))]
        arrivals["a", stream, way, s] = send.copy(source, target, z_device(way))

    def a_sum(stream):
        total = ext[spot(0, stream), PART_A]
        for way in (1, -1):
            last = (stream, way, HOPS[stream, way] - 1)
            arrivals.wait(("a",) + last)
            total = total + a_recv[slots["a"][last]]
        a_side[stream] = total
        if stream > 0:
            source, target = a_side.at[stream], a_side.at[NY + stream]
            arrivals["side", stream] = send.copy(source, target, y_device(stream))

    def finish_a():
        total = a_side[0]
        for stream in (1, 3, 2):
            arrivals.wait(("side", stream))
            total = total + a_side[NY + stream]
        done_a(total)

    def b_send(offset, way, step, source):
        target = b_recv.at[take("b", (offset, way, step))]
        arrivals["b", offset, way, step] = send.copy(source, target, y_device(way))

    def b_far(offset):
        way = 1 if offset % 2 == 0 else -1
        b_send(offset, way, 0, ext.at[spot(offset, 2), PART_B])
        b_send(offset, -way, 0, ext.at[spot(offset, -way), PART_B])

    def b_near(offset):
        way = 1 if offset % 2 == 0 else -1
        arrivals.wait(("b", offset, way, 0))
        held = slots["b"][offset, way, 0]
        b_recv[held] += ext[spot(offset, way), PART_B]
        b_send(offset, way, 1, b_recv.at[held])

    def b_total(offset):
        way = 1 if offset % 2 == 0 else -1
        total = ext[spot(offset, 0), PART_B]
        for key in ((offset, way, 1), (offset, -way, 0)):
            arrivals.wait(("b",) + key)
            total = total + b_recv[slots["b"][key]]
        b_sum[offset % NZ] = total

    def c_step(away, way):
        slot = 2 * (away - 1) + (way < 0)
        part = pl.ds(half_of(way), HALF_B) if away == 4 else ALL_B
        if away < 4:
            arrivals.wait(("c", away + 1, way))
            part_held = pl.ds(half_of(way), HALF_B) if away == 3 else ALL_B
            b_sum[way * away % NZ, part_held] += c_recv[slot + 2, part_held]
        source, target = b_sum.at[way * away % NZ, part], c_recv.at[slot, part]
        arrivals["c", away, way] = send.copy(source, target, z_device(way))

    def finish_b():
        total = b_sum[0]
        for way in (1, -1):
            arrivals.wait(("c", 1, way))
            total = total + c_recv[(way < 0) + 0]
        done_b(total)

    steps = {
        "cut": cut, "a": a_step, "side": a_sum, "done_a": finish_a, "far": b_far,
        "near": b_near, "sum": b_total, "c": c_step, "done_b": finish_b,
    }
    waiting = True
    for name, *which in SCATTER_ORDER:
        if waiting and name != "cut":
            ready()
            waiting = False
        steps[name](*which)


def gather(held, send):
    arrivals = Arrivals()

    def z_copy(dz, dy, part, way):
        source, target = held.at[spot(dz, dy), part], held.at[spot(dz - way, dy), part]
        return send.copy(source, target, z_device(way))

    def y_copy(dz, dy, part, way):
        source, target = held.at[spot(dz, dy), part], held.at[spot(dz, dy - way), part]
        return send.copy(source, target, y_device(way))

    def a_first():
        for step in (1, 3, 2):
            arrivals["side", step] = y_copy(0, 0, PART_A, step)

    def a_step(stream, way, s):
        if s > 0:
            arrivals.wait(("a", stream, way, s - 1))
        elif stream > 0:
            arrivals.wait(("side", stream))
        arrivals["a", stream, way, s] = z_copy(-way * s, -stream, PART_A, way)

    def a_end(stream, way):
        hops = HOPS[stream, way]
        arrivals.wait(("a", stream, way, hops - 1))

    def c_step(away, way):
        part = pl.ds(ROWS_A + half_of(way), HALF_B) if away == 4 else PART_B
        if away > 1:
            arrivals.wait(("c", away - 1, way))
        arrivals["c", away, way] = z_copy(-way * (away - 1), 0, part, way)

    def b_first(offset):
        if offset == 4:
            arrivals.wait(("c", 4, 1))
            arrivals.wait(("c", 4, -1))
        elif offset != 0:
            arrivals.wait(("c", abs(offset), 1 if offset < 0 else -1))
        for way in (1, -1):
            arrivals["b", offset, way] = y_copy(offset, 0, PART_B, way)

    def b_second(offset):
        way = 1 if offset % 2 == 0 else -1
        arrivals.wait(("b", offset, way))
        arrivals["b", offset, 2] = y_copy(offset, -way, PART_B, way)

    def b_end(offset):
        way = 1 if offset % 2 == 0 else -1
        arrivals.wait(("b", offset, -way))
        arrivals.wait(("b", offset, 2))

    steps = {
        "a_first": a_first, "a": a_step, "a_end": a_end, "c": c_step,
        "first": b_first, "second": b_second, "end": b_end,
    }
    for name, *which in GATHER_ORDER:
        steps[name](*which)


def split(value):
    high = value.astype(jnp.bfloat16)
    low = (value - high.astype(jnp.float32)).astype(jnp.bfloat16)
    return high, low


def mxu(a, b):
    return jnp.dot(a, b, preferred_element_type=jnp.float32)


def transform(fields, tables, right, left):
    halves = []
    for field in fields:
        high, low = split(jnp.concatenate(field, 1))
        halves.append(
            mxu(high, tables[right, 0])
            + (mxu(low, tables[right, 0]) + mxu(high, tables[right, 1]))
        )
    done = []
    for half in halves:
        high, low = split(jnp.concatenate([half[:, :W], half[:, W:]], 0))
        both = mxu(tables[left, 0], jnp.concatenate([high, low], 1))
        whole = both[:, :W] + (both[:, W:] + mxu(tables[left, 1], high))
        done.append((whole[:W], whole[W:]))
    return done


STEP, STEP_BACK, DFT, DFT_BACK = (0, 1), (1, 0), (2, 3), (3, 2)


def chain(trans, trans_ready, probe, counts, tables, waves, grads, own, grad_done):
    fields = [(probe[0, m], probe[1, m]) for m in range(MODES)]
    for j in range(DEPTH):
        trans_ready(j)
        tr, ti = trans[j, 0], trans[j, 1]
        entering = []
        for m, (real, imag) in enumerate(fields):
            waves[j, m, 0] = real
            waves[j, m, 1] = imag
            entering.append((tr * real - ti * imag, tr * imag + ti * real))
        fields = transform(entering, tables, *(STEP if j < DEPTH - 1 else DFT))
    intensity = sum(real * real + imag * imag for real, imag in fields)
    residual = intensity - count_scale * counts[0].astype(jnp.float32)
    residual = (4.0 * loss_scale) * residual
    fields = [(residual * real, residual * imag) for real, imag in fields]
    for j in reversed(range(DEPTH)):
        fields = transform(fields, tables, *(STEP_BACK if j < DEPTH - 1 else DFT_BACK))
        tr, ti = trans[j, 0], trans[j, 1]
        leaving, phase_part, absorb_part = [], 0.0, 0.0
        for m, (real, imag) in enumerate(fields):
            real, imag = tr * real + ti * imag, tr * imag - ti * real
            wr, wi = waves[j, m, 0], waves[j, m, 1]
            phase_part = phase_part + (wr * imag - wi * real)
            absorb_part = absorb_part - (wr * real + wi * imag)
            leaving.append((real, imag))
        fields = leaving
        target = grads.at[j] if j > 0 else own
        for rows_in, kind, rows_of in BANDS:
            target[rows_in] = (phase_part, absorb_part)[kind][rows_of]
        grad_done(j)


def main_kernel(
    rows_hbm, cols_hbm, slots_hbm, phase, absorb, probe_hbm, counts_hbm, tables_hbm,
    held,
    rows, cols, slots, probe, counts, tables,
    padded, ext, a_recv, a_side, b_recv, b_sum, c_recv,
    trans, waves, grads,
    load_sems, s_send, s_recv, g_send, g_recv, t_send, t_recv, d_send, d_recv,
):
    me = lax.axis_index("tile")
    d = lax.axis_index("depth")
    barrier = pltpu.get_barrier_semaphore()
    greeted = tile_partners()
    loads = [
        pltpu.make_async_copy(source, target, load_sems.at[i])
        for i, (source, target) in enumerate(
            [(rows_hbm, rows), (cols_hbm, cols), (slots_hbm, slots)]
            + [
                (tile.at[0, 0, :, pl.ds(c * W, W)], padded.at[m, c + 1, pl.ds(W, TS)])
                for m, tile in enumerate((phase, absorb))
                for c in range(TS // W)
            ]
            + [(probe_hbm, probe), (counts_hbm, counts), (tables_hbm, tables)]
        )
    ]
    for load in loads[:3]:
        load.start()
    for m in range(2):
        for c in range(CHUNKS):
            if 1 <= c <= TS // W:
                padded[m, c, :W] = jnp.zeros((W, W), jnp.float32)
                padded[m, c, W + TS :] = jnp.zeros((W, W), jnp.float32)
            else:
                padded[m, c] = jnp.zeros((PADDED, W), jnp.float32)
    for load in loads[3:9]:
        load.start()
    for partner in greeted:
        pl.semaphore_signal(barrier, inc=1, device_id=partner, device_id_type=MESH)

    @pl.when(d == 0)
    def _():
        for k in range(1, DEPTH):
            pl.semaphore_signal(barrier, inc=1, device_id={"depth": k}, device_id_type=MESH)

    @pl.when(d != 0)
    def _():
        pl.semaphore_signal(barrier, inc=1, device_id={"depth": 0}, device_id_type=MESH)

    for load in loads[:9]:
        load.wait()
    top, left = tile_corner(slots, me)
    lane = lax.broadcasted_iota(jnp.int32, (W, W), 1)
    z, y = tile_place()

    def cut(dz, dy):
        p = turned(z, dz, NZ) * NY + turned(y, dy, NY)
        start = jnp.clip(rows[p] - top, -W, TS) + W
        column = jnp.clip(cols[p] - left, -W, TS) + W
        chunk = lax.shift_right_logical(column, 7)
        after = jnp.minimum(chunk + 1, CHUNKS - 1)
        shift = column - chunk * W
        back = lax.bitwise_and(W - shift, W - 1)
        for m in range(2):
            first = padded[m, chunk, pl.ds(start, W), :]
            second = padded[m, after, pl.ds(start, W), :]
            moved = pltpu.roll(jnp.where(lane >= shift, first, second), back, 1)
            for rows_in, kind, rows_of in BANDS:
                if kind == m:
                    ext[spot(dz, dy), rows_in] = moved[rows_of]

    def ready():
        pl.semaphore_wait(barrier, len(greeted) + jnp.where(d == 0, DEPTH - 1, 1))
        for load in loads[9:]:
            load.start()

    send = Sender(s_send, s_recv)

    def trans_copy(j, part):
        rows_of = pl.ds(0, PIXELS) if part == 0 else pl.ds(PIXELS, REST)
        return pltpu.make_async_remote_copy(
            src_ref=trans.at[j, :, rows_of],
            dst_ref=trans.at[j, :, rows_of],
            send_sem=t_send.at[part],
            recv_sem=t_recv.at[part, j],
            device_id={"depth": 0},
            device_id_type=MESH,
        )

    def done(part):
        def put(total):
            rows_of = slice(0, PIXELS) if part == 0 else slice(PIXELS, W)
            count = total.shape[0] // 2
            damping = jnp.exp(-total[count:])
            trans[d, 0, rows_of] = damping * jnp.cos(total[:count])
            trans[d, 1, rows_of] = damping * jnp.sin(total[:count])

            @pl.when(d != 0)
            def _():
                trans_copy(d, part).start()

        return put

    scatter(
        cut, ready, done(0), done(1), ext, a_recv, a_side, b_recv, b_sum, c_recv, send
    )

    def grad_copy(j):
        return pltpu.make_async_remote_copy(
            src_ref=grads.at[j],
            dst_ref=held.at[0],
            send_sem=d_send.at[j],
            recv_sem=d_recv.at[0],
            device_id={"depth": j},
            device_id_type=MESH,
        )

    @pl.when(d == 0)
    def _():
        for load in loads[9:]:
            load.wait()

        def trans_ready(j):
            if j > 0:
                for part in range(2):
                    pltpu.make_async_remote_copy(
                        src_ref=trans.at[j, :, pl.ds(part * PIXELS, (PIXELS, REST)[part])],
                        dst_ref=trans.at[j, :, pl.ds(part * PIXELS, (PIXELS, REST)[part])],
                        send_sem=t_send.at[part],
                        recv_sem=t_recv.at[part, j],
                        device_id={"depth": 1},
                        device_id_type=MESH,
                    ).wait_recv()

        def grad_done(j):
            if j > 0:
                grad_copy(j).start()

        chain(trans, trans_ready, probe, counts, tables, waves, grads, held.at[0], grad_done)

    @pl.when(d != 0)
    def _():
        for load in loads[9:]:
            load.wait()
        for part in range(2):
            trans_copy(d, part).wait_send()
        pltpu.make_async_remote_copy(
            src_ref=held.at[0],
            dst_ref=held.at[0],
            send_sem=d_send.at[0],
            recv_sem=d_recv.at[0],
            device_id={"depth": 0},
            device_id_type=MESH,
        ).wait_recv()

    send_back = Sender(g_send, g_recv)
    gather(held, send_back)

    @pl.when(d == 0)
    def _():
        for j in range(1, DEPTH):
            grad_copy(j).wait_send()

    send.finish()
    send_back.finish()


def local(phase, absorb, probe, row_offsets, col_offsets, tile_slot, counts):
    f32 = jnp.float32
    mib = 1 << 20
    dma = pltpu.SemaphoreType.DMA
    tables = jnp.asarray(make_tables())
    gathered = pl.pallas_call(
        main_kernel,
        out_shape=jax.ShapeDtypeStruct((POS, BOTH, W), f32),
        in_specs=[HBM] * 8,
        out_specs=VMEM,
        scratch_shapes=[
            pltpu.SMEM((POS,), jnp.int32),
            pltpu.SMEM((POS,), jnp.int32),
            pltpu.SMEM((POS,), jnp.int32),
            pltpu.VMEM(probe.shape, f32),
            pltpu.VMEM(counts.shape, jnp.int32),
            pltpu.VMEM(tables.shape, jnp.bfloat16),
            pltpu.VMEM((2, CHUNKS, PADDED, W), f32),
            pltpu.VMEM((POS, BOTH, W), f32),
            pltpu.VMEM((28, ROWS_A, W), f32),
            pltpu.VMEM((2 * NY, ROWS_A, W), f32),
            pltpu.VMEM((24, ROWS_B, W), f32),
            pltpu.VMEM((NZ, ROWS_B, W), f32),
            pltpu.VMEM((8, ROWS_B, W), f32),
            pltpu.VMEM((DEPTH, 2, W, W), f32),
            pltpu.VMEM((DEPTH, MODES, 2, W, W), f32),
            pltpu.VMEM((DEPTH, BOTH, W), f32),
            dma((12,)),
            dma((SCATTER_COPIES,)),
            dma((SCATTER_COPIES,)),
            dma((GATHER_COPIES,)),
            dma((GATHER_COPIES,)),
            dma((2,)),
            dma((2, DEPTH)),
            dma((DEPTH,)),
            dma((1,)),
        ],
        compiler_params=pltpu.CompilerParams(
            collective_id=0, has_side_effects=True, vmem_limit_bytes=40 * mib
        ),
        name="main",
    )(*(
        pltpu.with_memory_space_constraint(v, pltpu.HBM)
        for v in (row_offsets, col_offsets, tile_slot, phase, absorb, probe, counts, tables)
    ))
    return pl.pallas_call(
        deposit_kernel,
        out_shape=(jax.ShapeDtypeStruct((1, 1, TS, TS), f32),) * 2,
        in_specs=[SMEM, SMEM, SMEM, VMEM],
        out_specs=(HBM, HBM),
        scratch_shapes=[
            pltpu.VMEM((2, CHUNKS, PADDED, W), f32),
            pltpu.SMEM((POS,), jnp.int32),
            dma((2 * (CHUNKS - 2),)),
        ],
        compiler_params=pltpu.CompilerParams(vmem_limit_bytes=24 * mib),
        name="deposit",
    )(row_offsets, col_offsets, tile_slot, gathered)


def solution(mesh):
    in_specs = (
        P("depth", "tile", None, None),
        P("depth", "tile", None, None),
        P(),
        P(),
        P(),
        P(),
        P("tile", None, None),
    )
    out_specs = (P("depth", "tile", None, None), P("depth", "tile", None, None))
    return jax.shard_map(local, mesh=mesh, in_specs=in_specs, out_specs=out_specs, check_vma=False)
```

```python
import functools
import math

import numpy as np
import jax
import jax.numpy as jnp
from jax import lax
from jax.experimental import pallas as pl
from jax.experimental.pallas import tpu as pltpu
from jax.sharding import PartitionSpec as P

W = 128
MODES = 4
TS = 384
GY = 4
POS = 32
NZ = 8
NY = 4
DEPTH = 8
BOTH = 2 * W
PIXELS = 56
ROWS_A = 2 * PIXELS
ROWS_B = BOTH - ROWS_A
HALF_B = ROWS_B // 2
REST = W - PIXELS
BANDS = (
    (slice(0, PIXELS), 0, slice(0, PIXELS)),
    (slice(PIXELS, ROWS_A), 1, slice(0, PIXELS)),
    (slice(ROWS_A, ROWS_A + REST), 0, slice(PIXELS, W)),
    (slice(ROWS_A + REST, BOTH), 1, slice(PIXELS, W)),
)
CHUNKS = TS // W + 2
PADDED = TS + 2 * W

count_scale = 0.0078125
loss_scale = 0.03125
fresnel_strength = 40.0

VMEM = pl.BlockSpec(memory_space=pltpu.VMEM)
SMEM = pl.BlockSpec(memory_space=pltpu.SMEM)
HBM = pl.BlockSpec(memory_space=pltpu.HBM)
ANY = pl.BlockSpec(memory_space=pl.ANY)
MESH = pl.DeviceIdType.MESH


def make_tables():
    index = np.arange(W)
    angle = 2.0 * np.pi * ((index[:, None] * index[None, :]) % W) / W
    dft = np.exp(-1j * angle) / math.sqrt(W)
    signed = ((index + W // 2) % W - W // 2) / W
    chirp = np.exp(-1j * fresnel_strength * signed**2)
    step = np.conj(dft) @ (chirp[:, None] * dft)
    tables = []
    for g in (step, dft):
        right = np.block([[g.real, g.imag], [-g.imag, g.real]])
        for table in (right, right.T):
            table = table.astype(np.float32)
            high = table.astype(jnp.bfloat16)
            low = (table - high.astype(np.float32)).astype(jnp.bfloat16)
            tables.append(np.stack([high, low]))
    return np.stack(tables)


def tile_corner(slots, me):
    def look(i, place):
        return jnp.where(slots[i] == me, i, place)

    place = lax.fori_loop(0, POS, look, jnp.int32(0))
    row = lax.shift_right_logical(place, 2)
    return row * TS, (place - row * GY) * TS


def overlap(rows, cols, p, top, left):
    dr = rows[p] - top
    dc = cols[p] - left
    return dr, dc, (dr > -W) & (dr < TS) & (dc > -W) & (dc < TS)


def deposit_kernel(rows, cols, slots, grads, phase_out, absorb_out, acc, found, sems):
    me = lax.axis_index("tile")
    top, left = tile_corner(slots, me)
    z, y = tile_place()
    lane = lax.broadcasted_iota(jnp.int32, (W, W), 1)

    def look(p, count):
        found[count] = p
        dr, dc, touches = overlap(rows, cols, p, top, left)
        return count + jnp.where(touches, 1, 0)

    count = lax.fori_loop(0, POS, look, jnp.int32(0))
    copies = []
    for m, target in enumerate((phase_out, absorb_out)):
        acc[m, 1 : CHUNKS - 1, W : W + TS] = jnp.zeros((CHUNKS - 2, TS, W), jnp.float32)

        def one(i, carry, m=m):
            p = found[i]
            row = lax.shift_right_logical(p, 2)
            place = turned(row, -z, NZ) * NY + turned(p - row * NY, -y, NY)
            start = rows[p] - top + W
            column = cols[p] - left + W
            chunk = lax.shift_right_logical(column, 7)
            shift = column - chunk * W
            pieces = [grads[place, rows_in] for rows_in, kind, _ in BANDS if kind == m]
            moved = pltpu.roll(jnp.concatenate(pieces, 0), shift, 1)
            acc[m, chunk, pl.ds(start, W), :] += jnp.where(lane >= shift, moved, 0.0)
            acc[m, chunk + 1, pl.ds(start, W), :] += jnp.where(lane < shift, moved, 0.0)
            return carry

        lax.fori_loop(0, count, one, 0)
        for c in range(TS // W):
            copy = pltpu.make_async_copy(
                acc.at[m, c + 1, pl.ds(W, TS)],
                target.at[0, 0, :, pl.ds(c * W, W)],
                sems.at[len(copies)],
            )
            copy.start()
            copies.append(copy)
    for copy in copies:
        copy.wait()


def tile_place():
    me = lax.axis_index("tile")
    z = me // NY
    return z, me - z * NY


def turned(value, step, count):
    return lax.rem(value + step + count, count)


def z_device(way):
    z, y = tile_place()
    return {"tile": turned(z, way, NZ) * NY + y}


def y_device(step):
    z, y = tile_place()
    return {"tile": z * NY + turned(y, step, NY)}


def tile_partners():
    return [z_device(k) for k in (1, -1, 2, -2)] + [y_device(k) for k in range(1, NY)]


class Sender:
    def __init__(self, send_sems, recv_sems):
        self.send_sems, self.recv_sems = send_sems, recv_sems
        self.started = []
        self.settled = 0

    def copy(self, source, target, device):
        n = len(self.started)
        copy = pltpu.make_async_remote_copy(
            src_ref=source,
            dst_ref=target,
            send_sem=self.send_sems.at[n],
            recv_sem=self.recv_sems.at[n],
            device_id=device,
            device_id_type=MESH,
        )
        copy.start()
        self.started.append(copy)
        return copy

    def settle(self, lag):
        while self.settled < len(self.started) - lag:
            self.started[self.settled].wait_send()
            self.settled += 1

    def finish(self):
        for copy in self.started[self.settled :]:
            copy.wait_send()


HOPS = {
    (0, 1): 4, (1, 1): 4, (2, -1): 4, (3, -1): 4, (2, 1): 3, (3, 1): 3, (0, -1): 3, (1, -1): 3,
}
SCATTER_ORDER = (
    ("cut", 4, 2), ("cut", 4, 1), ("a", 1, 1, 0), ("cut", 4, 3), ("far", 4), ("cut", 2, 2),
    ("cut", 3, 3), ("a", 3, -1, 0), ("cut", -3, 1), ("cut", -3, 2), ("cut", -1, 2),
    ("a", 3, 1, 0), ("a", 2, -1, 0), ("cut", -3, 0), ("cut", 3, 2), ("cut", 3, 1), ("cut", -1, 1),
    ("far", 3), ("cut", 1, 2), ("cut", 4, 0), ("cut", 1, 3), ("cut", 0, 1), ("cut", 0, 0),
    ("a", 1, -1, 0), ("cut", -2, 1), ("far", -3), ("a", 1, 1, 1), ("cut", -3, 3), ("cut", 2, 3),
    ("a", 0, -1, 0), ("near", 4), ("a", 0, 1, 0), ("cut", 2, 0), ("cut", -2, 2), ("cut", -2, 3),
    ("cut", -2, 0), ("cut", 3, 0), ("a", 3, 1, 1), ("cut", 1, 1), ("a", 2, 1, 0), ("cut", 2, 1),
    ("a", 2, -1, 1), ("far", -2), ("near", 3), ("a", 1, -1, 1), ("cut", -1, 0), ("a", 3, -1, 1),
    ("near", -3), ("far", 2), ("a", 1, 1, 2), ("cut", 0, 2), ("a", 0, 1, 1), ("a", 0, -1, 1),
    ("sum", 4), ("far", 1), ("c", 4, -1), ("c", 4, 1), ("a", 2, -1, 2), ("near", -2),
    ("a", 2, 1, 1), ("a", 1, -1, 2), ("near", 2), ("a", 3, 1, 2), ("sum", 3), ("cut", -1, 3),
    ("a", 3, -1, 2), ("far", -1), ("cut", 0, 3), ("a", 1, 1, 3), ("c", 3, 1), ("far", 0),
    ("sum", -3), ("c", 3, -1), ("cut", 1, 0), ("sum", -2), ("near", 1), ("a", 2, -1, 3),
    ("a", 2, 1, 2), ("a", 3, -1, 3), ("a", 0, 1, 2), ("near", -1), ("sum", 2), ("c", 2, -1),
    ("c", 2, 1), ("side", 1), ("sum", 1), ("near", 0), ("side", 2), ("a", 0, -1, 2), ("side", 3),
    ("a", 0, 1, 3), ("sum", -1), ("c", 1, -1), ("c", 1, 1), ("side", 0), ("sum", 0), ("done_a",),
    ("done_b",),
)
GATHER_ORDER = (
    ("c", 1, -1), ("c", 1, 1), ("a_first",), ("a", 0, 1, 0), ("first", 0), ("a", 0, -1, 0),
    ("c", 2, -1), ("c", 2, 1), ("first", 1), ("a", 3, -1, 0), ("a", 1, -1, 0), ("first", -1),
    ("a", 2, -1, 0), ("second", 0), ("a", 1, 1, 0), ("a", 2, 1, 0), ("c", 3, 1), ("first", -2),
    ("second", 1), ("first", 2), ("a", 0, 1, 1), ("c", 3, -1), ("a", 0, -1, 1), ("a", 3, -1, 1),
    ("a", 1, 1, 1), ("a", 3, 1, 0), ("first", -3), ("c", 4, 1), ("a", 2, -1, 1), ("a", 0, 1, 2),
    ("second", -1), ("second", 2), ("c", 4, -1), ("a", 2, 1, 1), ("first", 3), ("end", 1),
    ("a", 1, -1, 1), ("a", 3, 1, 1), ("a", 2, -1, 2), ("a", 3, -1, 2), ("a", 1, 1, 2),
    ("first", 4), ("end", 0), ("a", 1, -1, 2), ("a", 0, 1, 3), ("end", -1), ("a", 2, 1, 2),
    ("second", -2), ("second", 3), ("a", 0, -1, 2), ("a", 1, 1, 3), ("a", 3, -1, 3),
    ("second", 4), ("second", -3), ("end", 2), ("a_end", 1, -1), ("a", 3, 1, 2), ("a", 2, -1, 3),
    ("end", -2), ("a_end", 0, -1), ("end", 3), ("a_end", 1, 1), ("end", -3), ("a_end", 0, 1),
    ("a_end", 3, -1), ("end", 4), ("a_end", 2, -1), ("a_end", 2, 1), ("a_end", 3, 1),
)
SCATTER_COPIES = 28 + 3 + 24 + 8
LAG = 24
GATHER_COPIES = 28 + 3 + 24 + 8
PART_A = pl.ds(0, ROWS_A)
PART_B = pl.ds(ROWS_A, ROWS_B)
ALL_B = pl.ds(0, ROWS_B)


def half_of(way):
    return 0 if way == 1 else HALF_B


def spot(dz, dy):
    return (dz % NZ) * NY + dy % NY


class Arrivals:
    def __init__(self):
        self.copies, self.seen = {}, set()

    def __setitem__(self, key, copy):
        self.copies[key] = copy

    def wait(self, key):
        if key not in self.seen:
            self.copies[key].wait_recv()
            self.seen.add(key)
            return True
        return False


def scatter(cut, ready, done_a, done_b, ext, a_recv, a_side, b_recv, b_sum, c_recv, send):
    arrivals = Arrivals()
    slots = {}

    def take(kind, key):
        used = slots.setdefault(kind, {})
        used[key] = len(used)
        return used[key]

    def a_step(stream, way, s):
        dest = spot(way * (HOPS[stream, way] - s), stream)
        if s > 0:
            arrivals.wait(("a", stream, way, s - 1))
            held = slots["a"][stream, way, s - 1]
            a_recv[held] += ext[dest, PART_A]
            source = a_recv.at[held]
        else:
            source = ext.at[dest, PART_A]
        target = a_recv.at[take("a", (stream, way, s))]
        arrivals["a", stream, way, s] = send.copy(source, target, z_device(way))

    def a_sum(stream):
        total = ext[spot(0, stream), PART_A]
        for way in (1, -1):
            last = (stream, way, HOPS[stream, way] - 1)
            arrivals.wait(("a",) + last)
            total = total + a_recv[slots["a"][last]]
        a_side[stream] = total
        if stream > 0:
            source, target = a_side.at[stream], a_side.at[NY + stream]
            arrivals["side", stream] = send.copy(source, target, y_device(stream))

    def finish_a():
        total = a_side[0]
        for stream in (1, 3, 2):
            arrivals.wait(("side", stream))
            total = total + a_side[NY + stream]
        done_a(total)

    def b_send(offset, way, step, source):
        target = b_recv.at[take("b", (offset, way, step))]
        arrivals["b", offset, way, step] = send.copy(source, target, y_device(way))

    def b_far(offset):
        way = 1 if offset % 2 == 0 else -1
        b_send(offset, way, 0, ext.at[spot(offset, 2), PART_B])
        b_send(offset, -way, 0, ext.at[spot(offset, -way), PART_B])

    def b_near(offset):
        way = 1 if offset % 2 == 0 else -1
        arrivals.wait(("b", offset, way, 0))
        held = slots["b"][offset, way, 0]
        b_recv[held] += ext[spot(offset, way), PART_B]
        b_send(offset, way, 1, b_recv.at[held])

    def b_total(offset):
        way = 1 if offset % 2 == 0 else -1
        total = ext[spot(offset, 0), PART_B]
        for key in ((offset, way, 1), (offset, -way, 0)):
            arrivals.wait(("b",) + key)
            total = total + b_recv[slots["b"][key]]
        b_sum[offset % NZ] = total

    def c_step(away, way):
        slot = 2 * (away - 1) + (way < 0)
        part = pl.ds(half_of(way), HALF_B) if away == 4 else ALL_B
        if away < 4:
            arrivals.wait(("c", away + 1, way))
            part_held = pl.ds(half_of(way), HALF_B) if away == 3 else ALL_B
            b_sum[way * away % NZ, part_held] += c_recv[slot + 2, part_held]
        source, target = b_sum.at[way * away % NZ, part], c_recv.at[slot, part]
        arrivals["c", away, way] = send.copy(source, target, z_device(way))

    def finish_b():
        total = b_sum[0]
        for way in (1, -1):
            arrivals.wait(("c", 1, way))
            total = total + c_recv[(way < 0) + 0]
        done_b(total)

    steps = {
        "cut": cut, "a": a_step, "side": a_sum, "done_a": finish_a, "far": b_far,
        "near": b_near, "sum": b_total, "c": c_step, "done_b": finish_b,
    }
    waiting = True
    for name, *which in SCATTER_ORDER:
        if waiting and name != "cut":
            ready()
            waiting = False
        steps[name](*which)
        send.settle(LAG)


def gather(held, send):
    arrivals = Arrivals()

    def z_copy(dz, dy, part, way):
        source, target = held.at[spot(dz, dy), part], held.at[spot(dz - way, dy), part]
        return send.copy(source, target, z_device(way))

    def y_copy(dz, dy, part, way):
        source, target = held.at[spot(dz, dy), part], held.at[spot(dz, dy - way), part]
        return send.copy(source, target, y_device(way))

    def a_first():
        for step in (1, 3, 2):
            arrivals["side", step] = y_copy(0, 0, PART_A, step)

    def a_step(stream, way, s):
        if s > 0:
            arrivals.wait(("a", stream, way, s - 1))
        elif stream > 0:
            arrivals.wait(("side", stream))
        arrivals["a", stream, way, s] = z_copy(-way * s, -stream, PART_A, way)

    def a_end(stream, way):
        hops = HOPS[stream, way]
        arrivals.wait(("a", stream, way, hops - 1))

    def c_step(away, way):
        part = pl.ds(ROWS_A + half_of(way), HALF_B) if away == 4 else PART_B
        if away > 1:
            arrivals.wait(("c", away - 1, way))
        arrivals["c", away, way] = z_copy(-way * (away - 1), 0, part, way)

    def b_first(offset):
        if offset == 4:
            arrivals.wait(("c", 4, 1))
            arrivals.wait(("c", 4, -1))
        elif offset != 0:
            arrivals.wait(("c", abs(offset), 1 if offset < 0 else -1))
        for way in (1, -1):
            arrivals["b", offset, way] = y_copy(offset, 0, PART_B, way)

    def b_second(offset):
        way = 1 if offset % 2 == 0 else -1
        arrivals.wait(("b", offset, way))
        arrivals["b", offset, 2] = y_copy(offset, -way, PART_B, way)

    def b_end(offset):
        way = 1 if offset % 2 == 0 else -1
        arrivals.wait(("b", offset, -way))
        arrivals.wait(("b", offset, 2))

    steps = {
        "a_first": a_first, "a": a_step, "a_end": a_end, "c": c_step,
        "first": b_first, "second": b_second, "end": b_end,
    }
    for name, *which in GATHER_ORDER:
        steps[name](*which)
        send.settle(LAG)


def split(value):
    high = value.astype(jnp.bfloat16)
    low = (value - high.astype(jnp.float32)).astype(jnp.bfloat16)
    return high, low


def mxu(a, b):
    return jnp.dot(a, b, preferred_element_type=jnp.float32)


def transform(fields, tables, right, left):
    halves = []
    for field in fields:
        high, low = split(jnp.concatenate(field, 1))
        both = mxu(jnp.concatenate([high, low], 0), tables[right, 0])
        halves.append(both[:W] + (both[W:] + mxu(high, tables[right, 1])))
    done = []
    for half in halves:
        high, low = split(jnp.concatenate([half[:, :W], half[:, W:]], 0))
        both = mxu(tables[left, 0], jnp.concatenate([high, low], 1))
        whole = both[:, :W] + (both[:, W:] + mxu(tables[left, 1], high))
        done.append((whole[:W], whole[W:]))
    return done


def cos_sin(phase):
    half = 0.5 * phase
    square = half * half
    sine, cosine = 0.0, 0.0
    for k in reversed(range(7)):
        cosine = cosine * square + (-1.0) ** k / math.factorial(2 * k)
        sine = sine * square + (-1.0) ** k / math.factorial(2 * k + 1)
    sine = sine * half
    return 1.0 - 2.0 * sine * sine, 2.0 * sine * cosine


STEP, STEP_BACK, DFT, DFT_BACK = (0, 1), (1, 0), (2, 3), (3, 2)


def chain(trans, trans_ready, probe, counts, tables, waves, grads, own, grad_done):
    fields = [(probe[0, m], probe[1, m]) for m in range(MODES)]
    for j in range(DEPTH):
        trans_ready(j)
        tr, ti = trans[j, 0], trans[j, 1]
        entering = []
        for m, (real, imag) in enumerate(fields):
            waves[j, m, 0] = real
            waves[j, m, 1] = imag
            entering.append((tr * real - ti * imag, tr * imag + ti * real))
        fields = transform(entering, tables, *(STEP if j < DEPTH - 1 else DFT))
    intensity = sum(real * real + imag * imag for real, imag in fields)
    residual = intensity - count_scale * counts[0].astype(jnp.float32)
    residual = (4.0 * loss_scale) * residual
    fields = [(residual * real, residual * imag) for real, imag in fields]
    for j in reversed(range(DEPTH)):
        fields = transform(fields, tables, *(STEP_BACK if j < DEPTH - 1 else DFT_BACK))
        tr, ti = trans[j, 0], trans[j, 1]
        leaving, phase_part, absorb_part = [], 0.0, 0.0
        for m, (real, imag) in enumerate(fields):
            real, imag = tr * real + ti * imag, tr * imag - ti * real
            wr, wi = waves[j, m, 0], waves[j, m, 1]
            phase_part = phase_part + (wr * imag - wi * real)
            absorb_part = absorb_part - (wr * real + wi * imag)
            leaving.append((real, imag))
        fields = leaving
        target = grads.at[j] if j > 0 else own
        for rows_in, kind, rows_of in BANDS:
            target[rows_in] = (phase_part, absorb_part)[kind][rows_of]
        grad_done(j)


def main_kernel(
    rows_hbm, cols_hbm, slots_hbm, phase, absorb, probe_hbm, counts_hbm, tables_hbm,
    held,
    rows, cols, slots, probe, counts, tables,
    padded, ext, a_recv, a_side, b_recv, b_sum, c_recv,
    trans, waves, grads,
    load_sems, s_send, s_recv, g_send, g_recv, t_send, t_recv, d_send, d_recv,
):
    me = lax.axis_index("tile")
    d = lax.axis_index("depth")
    barrier = pltpu.get_barrier_semaphore()
    greeted = tile_partners()
    loads = [
        pltpu.make_async_copy(source, target, load_sems.at[i])
        for i, (source, target) in enumerate(
            [(rows_hbm, rows), (cols_hbm, cols), (slots_hbm, slots)]
            + [
                (tile.at[0, 0, :, pl.ds(c * W, W)], padded.at[m, c + 1, pl.ds(W, TS)])
                for m, tile in enumerate((phase, absorb))
                for c in range(TS // W)
            ]
            + [(probe_hbm, probe), (counts_hbm, counts), (tables_hbm, tables)]
        )
    ]
    for load in loads[:3]:
        load.start()
    for m in range(2):
        for c in range(CHUNKS):
            if 1 <= c <= TS // W:
                padded[m, c, :W] = jnp.zeros((W, W), jnp.float32)
                padded[m, c, W + TS :] = jnp.zeros((W, W), jnp.float32)
            else:
                padded[m, c] = jnp.zeros((PADDED, W), jnp.float32)
    for load in loads[3:9]:
        load.start()
    for partner in greeted:
        pl.semaphore_signal(barrier, inc=1, device_id=partner, device_id_type=MESH)

    @pl.when(d == 0)
    def _():
        for k in range(1, DEPTH):
            pl.semaphore_signal(barrier, inc=1, device_id={"depth": k}, device_id_type=MESH)

    @pl.when(d != 0)
    def _():
        pl.semaphore_signal(barrier, inc=1, device_id={"depth": 0}, device_id_type=MESH)

    for load in loads[:9]:
        load.wait()
    top, left = tile_corner(slots, me)
    lane = lax.broadcasted_iota(jnp.int32, (W, W), 1)
    z, y = tile_place()

    def cut(dz, dy):
        p = turned(z, dz, NZ) * NY + turned(y, dy, NY)
        start = jnp.clip(rows[p] - top, -W, TS) + W
        column = jnp.clip(cols[p] - left, -W, TS) + W
        chunk = lax.shift_right_logical(column, 7)
        after = jnp.minimum(chunk + 1, CHUNKS - 1)
        shift = column - chunk * W
        back = lax.bitwise_and(W - shift, W - 1)
        for m in range(2):
            first = padded[m, chunk, pl.ds(start, W), :]
            second = padded[m, after, pl.ds(start, W), :]
            moved = pltpu.roll(jnp.where(lane >= shift, first, second), back, 1)
            for rows_in, kind, rows_of in BANDS:
                if kind == m:
                    ext[spot(dz, dy), rows_in] = moved[rows_of]

    def ready():
        pl.semaphore_wait(barrier, len(greeted) + jnp.where(d == 0, DEPTH - 1, 1))
        for load in loads[9:]:
            load.start()

    send = Sender(s_send, s_recv)

    def trans_copy(j, part):
        rows_of = pl.ds(0, PIXELS) if part == 0 else pl.ds(PIXELS, REST)
        return pltpu.make_async_remote_copy(
            src_ref=trans.at[j, :, rows_of],
            dst_ref=trans.at[j, :, rows_of],
            send_sem=t_send.at[part],
            recv_sem=t_recv.at[part, j],
            device_id={"depth": 0},
            device_id_type=MESH,
        )

    def done(part):
        def put(total):
            rows_of = slice(0, PIXELS) if part == 0 else slice(PIXELS, W)
            count = total.shape[0] // 2
            damping = jnp.exp(-total[count:])
            cosine, sine = cos_sin(total[:count])
            trans[d, 0, rows_of] = damping * cosine
            trans[d, 1, rows_of] = damping * sine

            @pl.when(d != 0)
            def _():
                trans_copy(d, part).start()

        return put

    scatter(
        cut, ready, done(0), done(1), ext, a_recv, a_side, b_recv, b_sum, c_recv, send
    )

    def grad_copy(j):
        return pltpu.make_async_remote_copy(
            src_ref=grads.at[j],
            dst_ref=held.at[0],
            send_sem=d_send.at[j],
            recv_sem=d_recv.at[0],
            device_id={"depth": j},
            device_id_type=MESH,
        )

    @pl.when(d == 0)
    def _():
        for load in loads[9:]:
            load.wait()

        def trans_ready(j):
            if j == 1:
                send.finish()
            if j > 0:
                for part in range(2):
                    pltpu.make_async_remote_copy(
                        src_ref=trans.at[j, :, pl.ds(part * PIXELS, (PIXELS, REST)[part])],
                        dst_ref=trans.at[j, :, pl.ds(part * PIXELS, (PIXELS, REST)[part])],
                        send_sem=t_send.at[part],
                        recv_sem=t_recv.at[part, j],
                        device_id={"depth": 1},
                        device_id_type=MESH,
                    ).wait_recv()

        def grad_done(j):
            if j > 0:
                grad_copy(j).start()

        chain(trans, trans_ready, probe, counts, tables, waves, grads, held.at[0], grad_done)

    @pl.when(d != 0)
    def _():
        for load in loads[9:]:
            load.wait()
        send.finish()
        for part in range(2):
            trans_copy(d, part).wait_send()
        pltpu.make_async_remote_copy(
            src_ref=held.at[0],
            dst_ref=held.at[0],
            send_sem=d_send.at[0],
            recv_sem=d_recv.at[0],
            device_id={"depth": 0},
            device_id_type=MESH,
        ).wait_recv()

    send_back = Sender(g_send, g_recv)
    gather(held, send_back)

    @pl.when(d == 0)
    def _():
        for j in range(1, DEPTH):
            grad_copy(j).wait_send()

    send_back.finish()


def local(phase, absorb, probe, row_offsets, col_offsets, tile_slot, counts):
    f32 = jnp.float32
    mib = 1 << 20
    dma = pltpu.SemaphoreType.DMA
    tables = jnp.asarray(make_tables())
    gathered = pl.pallas_call(
        main_kernel,
        out_shape=jax.ShapeDtypeStruct((POS, BOTH, W), f32),
        in_specs=[HBM] * 8,
        out_specs=VMEM,
        scratch_shapes=[
            pltpu.SMEM((POS,), jnp.int32),
            pltpu.SMEM((POS,), jnp.int32),
            pltpu.SMEM((POS,), jnp.int32),
            pltpu.VMEM(probe.shape, f32),
            pltpu.VMEM(counts.shape, jnp.int32),
            pltpu.VMEM(tables.shape, jnp.bfloat16),
            pltpu.VMEM((2, CHUNKS, PADDED, W), f32),
            pltpu.VMEM((POS, BOTH, W), f32),
            pltpu.VMEM((28, ROWS_A, W), f32),
            pltpu.VMEM((2 * NY, ROWS_A, W), f32),
            pltpu.VMEM((24, ROWS_B, W), f32),
            pltpu.VMEM((NZ, ROWS_B, W), f32),
            pltpu.VMEM((8, ROWS_B, W), f32),
            pltpu.VMEM((DEPTH, 2, W, W), f32),
            pltpu.VMEM((DEPTH, MODES, 2, W, W), f32),
            pltpu.VMEM((DEPTH, BOTH, W), f32),
            dma((12,)),
            dma((SCATTER_COPIES,)),
            dma((SCATTER_COPIES,)),
            dma((GATHER_COPIES,)),
            dma((GATHER_COPIES,)),
            dma((2,)),
            dma((2, DEPTH)),
            dma((DEPTH,)),
            dma((1,)),
        ],
        compiler_params=pltpu.CompilerParams(
            collective_id=0, has_side_effects=True, vmem_limit_bytes=40 * mib
        ),
        name="main",
    )(*(
        pltpu.with_memory_space_constraint(v, pltpu.HBM)
        for v in (row_offsets, col_offsets, tile_slot, phase, absorb, probe, counts, tables)
    ))
    return pl.pallas_call(
        deposit_kernel,
        out_shape=(jax.ShapeDtypeStruct((1, 1, TS, TS), f32),) * 2,
        in_specs=[SMEM, SMEM, SMEM, VMEM],
        out_specs=(HBM, HBM),
        scratch_shapes=[
            pltpu.VMEM((2, CHUNKS, PADDED, W), f32),
            pltpu.SMEM((POS,), jnp.int32),
            dma((2 * (CHUNKS - 2),)),
        ],
        compiler_params=pltpu.CompilerParams(vmem_limit_bytes=24 * mib),
        name="deposit",
    )(row_offsets, col_offsets, tile_slot, gathered)


def solution(mesh):
    in_specs = (
        P("depth", "tile", None, None),
        P("depth", "tile", None, None),
        P(),
        P(),
        P(),
        P(),
        P("tile", None, None),
    )
    out_specs = (P("depth", "tile", None, None), P("depth", "tile", None, None))
    return jax.shard_map(local, mesh=mesh, in_specs=in_specs, out_specs=out_specs, check_vma=False)
```
